128 devices in a mesh: dp: 16 (over x_lo, y, core), mp: 8 (over x_hi, z).
Axes of the slice: x: 4 (x_hi: 2, x_lo: 2; x = x_hi * 2 + x_lo), y: 4, z: 4, core: 2. Of those that a mesh axis runs over, the one named last changes fastest.
Arguments:
- pair_tokens: bfloat16 [256, 48, 8192], P('dp', None, 'mp'), may hold values from -6 to 6
- norm_gain: float32 [8192], replicated, may hold values from 0.1 to 1.9
- q_weight: bfloat16 [8192, 4096], P('dp', 'mp'), may hold values from -1.5 to 1.5
- k_weight: bfloat16 [8192, 1024], P('dp', 'mp'), may hold values from -1.5 to 1.5
- value_weight: bfloat16 [8192, 1024], P('dp', 'mp'), may hold values from -0.0625 to 0.0625
- o_weight: bfloat16 [4096, 8192], P('mp', 'dp'), may hold values from -0.375 to 0.375
- pair_row: int32 [256], replicated, may hold values from 0 to 63, as said below
- pair_span: int32 [256, 2], replicated, may hold values from 0 to 128, as said below
- block_ids: int32 [8192], P('dp'), may hold values from 0 to 11, as said below
Outputs:
- attn_out: bfloat16 [8192, 8192], P('dp', 'mp')
The draws below stay inside these ranges and needn't reach their ends.
Inputs may be any that keep to these rules, and one draw needn't show every extreme that they name: `pair_row`: every packed row is tiled exactly by the spans of the pairs that name it; the pairs listed on one index of dp that name rows of one index of dp number at most 1, and 1 is reached. `pair_span`: each span holds one pair, start before end; end - start is at least 3 and at most 48; 48 is reached in every row, and the last pair of every row ends at 128. `block_ids`: the pair's place counts the pairs of its row in order of position; roles are 0 prompt, 1 chosen, 2 rejected, in that order within each pair, each present; consistent with pair_row and pair_span.
All inputs are finite; a program needn't handle non-finite values.
Results may differ from the reference program's by a relative error of at most 0.013.
Values may be sent and summed in bfloat16 or wider, within the bound.
No kernel may reach another device: no remote copies, remote signals or barrier semaphores. Data moves between devices by JAX's collectives and lax.ppermute only.
A program may use at most 128 MiB of HBM per device.

```python
import jax
import jax.numpy as jnp
from jax import lax

MODEL_WIDTH = 8192
QUERY_HEADS = 32
KEY_VALUE_HEADS = 8
HEAD_SIZE = 128
ROW_TOKENS = 128
PAIR_CAP = 48
PAIRS_ROW = 4
PACK_ROWS = 4
QUERY_PER_KV = 4
ROWS = 64
TOKENS = 8192
PAIRS_DEV = 16
NPAIRS = 256
N_DP = 16
N_MP = 8


def packing_layout(key):
    key_rows = jax.random.split(jax.random.fold_in(key, 7), 7)
    count = PAIRS_ROW
    rest = ROW_TOKENS - PAIR_CAP
    shortest = rest // 4
    spare = rest - (count - 1) * shortest
    cuts = jnp.sort(jax.random.randint(key_rows[0], (ROWS, count - 2), 0, spare + 1), axis=1)
    edges = jnp.concatenate([jnp.zeros((ROWS, 1), jnp.int32), cuts, jnp.full((ROWS, 1), spare, jnp.int32)], axis=1)
    others = edges[:, 1:] - edges[:, :-1] + shortest
    unordered = jnp.concatenate([jnp.full((ROWS, 1), PAIR_CAP, jnp.int32), others], axis=1)
    order_keys = jax.random.randint(key_rows[1], (ROWS, count), 0, 1 << 20) * count + jnp.arange(count)
    order = jnp.argsort(order_keys, axis=1)
    lengths = jnp.take_along_axis(unordered, order, axis=1)
    starts = jnp.cumsum(lengths, axis=1) - lengths
    prompt = 1 + jax.random.randint(key_rows[2], (ROWS, count), 0, lengths - 2)
    chosen = 1 + jax.random.randint(key_rows[3], (ROWS, count), 0, lengths - 1 - prompt)
    placing = jax.random.permutation(key_rows[4], N_DP)
    shift_all = jax.random.permutation(key_rows[5], N_DP)
    shifts = shift_all[jnp.arange(PAIRS_DEV) % N_DP]
    slot_keys = jax.random.randint(key_rows[6], (N_DP, PAIRS_DEV), 0, 1 << 20) * PAIRS_DEV + jnp.arange(PAIRS_DEV)[None, :]
    slot_of = jnp.argsort(slot_keys, axis=1)
    source = jnp.arange(NPAIRS) // PAIRS_DEV
    within_src = jnp.arange(NPAIRS) % PAIRS_DEV
    owner = (placing[source] + shifts[within_src]) % N_DP
    slot = slot_of[owner, within_src]
    row = owner * PACK_ROWS + slot // count
    place = slot % count
    return (row, starts, lengths, prompt, chosen, place)


def draw_pair_row(key, part):
    row, starts, lengths, prompt, chosen, place = packing_layout(key)
    return row.astype(jnp.int32)


def draw_pair_span(key, part):
    row, starts, lengths, prompt, chosen, place = packing_layout(key)
    first = starts[row, place]
    return jnp.stack([first, first + lengths[row, place]], axis=1).astype(jnp.int32)


def draw_block_ids(key, part):
    row, starts, lengths, prompt, chosen, place = packing_layout(key)
    steps_t = jnp.arange(ROW_TOKENS)
    which = jnp.sum((steps_t[None, :, None] >= starts[:, None, 1:]).astype(jnp.int32), axis=2)
    offset = steps_t[None, :] - jnp.take_along_axis(starts, which, axis=1)
    prompt_len = jnp.take_along_axis(prompt, which, axis=1)
    chosen_len = jnp.take_along_axis(chosen, which, axis=1)
    role = (offset >= prompt_len).astype(jnp.int32) + (offset >= prompt_len + chosen_len).astype(jnp.int32)
    return (3 * which + role).reshape(-1).astype(jnp.int32)


def projections(key):
    key_rows = jax.random.split(jax.random.fold_in(key, 11), 2)
    rotary_base = jnp.clip(jax.random.normal(key_rows[0], (MODEL_WIDTH, KEY_VALUE_HEADS * HEAD_SIZE), jnp.float32), -4.0, 4.0) * MODEL_WIDTH ** (-0.5)
    noise = jnp.clip(jax.random.normal(key_rows[1], (MODEL_WIDTH, QUERY_HEADS * HEAD_SIZE), jnp.float32), -4.0, 4.0) * MODEL_WIDTH ** (-0.5)
    return (rotary_base, noise)


def draw_k_weight(key, part):
    rotary_base, noise = projections(key)
    return rotary_base.astype(jnp.bfloat16)


def draw_q_weight(key, part):
    rotary_base, noise = projections(key)
    return noise.astype(jnp.bfloat16)


def block_scale(rng, shape, cuts, least, high):
    loudness = 1.0
    for dim, blocks in cuts:
        heights = jax.random.uniform(jax.random.fold_in(jax.random.fold_in(rng, 6), dim), (blocks,), jnp.float32, least / len(cuts), high / len(cuts))
        loudness = loudness * jnp.repeat(jnp.exp(heights), shape[dim] // blocks).reshape((-1,) + (1,) * (len(shape) - 1 - dim))
    return loudness


def normal_values(rng, extent, deviation, limit, pieces=(), kind=jnp.bfloat16):
    gain = block_scale(rng, extent, pieces, -0.22, 0.18) if pieces else 1.0
    values = jax.random.normal(rng, extent, jnp.float32) * deviation * gain
    return jnp.minimum(jnp.maximum(values, -limit), limit).astype(kind)


def setup_inputs(seed: int = 0) -> dict:
    key_of = jax.random.split(jax.random.key(seed), 10)
    return {
        "pair_tokens": normal_values(key_of[0], (NPAIRS, PAIR_CAP, MODEL_WIDTH), 1.0, 6.0, ((0, 16), (2, 8))),
        "norm_gain": jnp.clip(1.0 + 0.18 * jax.random.normal(key_of[1], (MODEL_WIDTH,), jnp.float32), 0.1, 1.9),
        "q_weight": draw_q_weight(jax.random.fold_in(key_of[9], 71), 0),
        "k_weight": draw_k_weight(jax.random.fold_in(key_of[9], 71), 0),
        "value_weight": normal_values(key_of[4], (MODEL_WIDTH, KEY_VALUE_HEADS * HEAD_SIZE), MODEL_WIDTH ** -0.5, 0.0625, ((0, 16), (1, 8))),
        "o_weight": normal_values(key_of[5], (QUERY_HEADS * HEAD_SIZE, MODEL_WIDTH), (QUERY_HEADS * HEAD_SIZE // 16) ** -0.5, 0.375, ((0, 8), (1, 16))),
        "pair_row": draw_pair_row(jax.random.fold_in(key_of[9], 71), 0),
        "pair_span": draw_pair_span(jax.random.fold_in(key_of[9], 71), 0),
        "block_ids": draw_block_ids(jax.random.fold_in(key_of[9], 71), 0),
    }


def apply_rotary(values, token_position, heads):
    half = HEAD_SIZE // 2
    freq = 500000.0 ** (-(jnp.arange(half, dtype=jnp.float32) * 2.0 / HEAD_SIZE))
    angle = token_position.astype(jnp.float32)[:, None] * freq[None, :]
    cosine = jnp.cos(angle)[:, None, :]
    sine = jnp.sin(angle)[:, None, :]
    shaped = values.reshape(values.shape[0], heads, HEAD_SIZE)
    first = shaped[..., :half]
    second = shaped[..., half:]
    turned = jnp.concatenate([first * cosine - second * sine, second * cosine + first * sine], axis=-1)
    return turned.reshape(values.shape[0], heads * HEAD_SIZE).astype(jnp.bfloat16)

def row_mask(ids):
    pair_of = ids // 3
    role_of = ids % 3
    steps_a = jnp.arange(ids.shape[0])
    causal = steps_a[None, :] <= steps_a[:, None]
    same = pair_of[:, None] == pair_of[None, :]
    hidden_pair = (role_of[:, None] == 2) & (role_of[None, :] == 1)
    return causal & same & jnp.logical_not(hidden_pair)

def reference(pair_tokens, norm_gain, q_weight, k_weight, value_weight, o_weight, pair_row, pair_span, block_ids):
    slots = jnp.arange(PAIR_CAP, dtype=jnp.int32)
    length = pair_span[:, 1] - pair_span[:, 0]
    target = pair_row[:, None] * ROW_TOKENS + pair_span[:, 0][:, None] + slots[None, :]
    target = jnp.where(slots[None, :] < length[:, None], target, TOKENS).astype(jnp.int32)
    packed = jnp.zeros((TOKENS, MODEL_WIDTH), jnp.bfloat16).at[target.reshape(-1)].set(pair_tokens.reshape(-1, MODEL_WIDTH), mode='drop')
    group_width = QUERY_HEADS * HEAD_SIZE // N_MP

    def one_row(inputs):
        row_tokens, ids = inputs
        visible = row_mask(ids)
        token_position = lax.optimization_barrier(jnp.sum(visible.astype(jnp.int32), axis=1)) - 1
        wide = row_tokens.astype(jnp.float32)
        scale = lax.rsqrt(lax.optimization_barrier(jnp.mean(wide * wide, axis=-1, keepdims=True)) + 1e-05)
        normed = (wide * scale * norm_gain[None, :]).astype(jnp.bfloat16)
        query_heads = jnp.dot(normed, q_weight, preferred_element_type=jnp.float32)
        key_rows = jnp.dot(normed, k_weight, preferred_element_type=jnp.float32)
        value_heads = jnp.dot(normed, value_weight, preferred_element_type=jnp.float32).astype(jnp.bfloat16)
        rotated_query = apply_rotary(query_heads, token_position, QUERY_HEADS).astype(jnp.float32).reshape(ROW_TOKENS, KEY_VALUE_HEADS, QUERY_PER_KV, HEAD_SIZE)
        rotated_key = apply_rotary(key_rows, token_position, KEY_VALUE_HEADS).astype(jnp.float32).reshape(ROW_TOKENS, KEY_VALUE_HEADS, HEAD_SIZE)
        value_expanded = value_heads.astype(jnp.float32).reshape(ROW_TOKENS, KEY_VALUE_HEADS, HEAD_SIZE)
        scores = jnp.einsum('ihgd,jhd->hgij', rotated_query, rotated_key) * HEAD_SIZE ** (-0.5)
        scores = jnp.where(visible[None, None], scores, -1e+30)
        top = lax.optimization_barrier(jnp.max(scores, axis=-1, keepdims=True))
        expo = jnp.exp(scores - top)
        probs = (expo / lax.optimization_barrier(jnp.sum(expo, axis=-1, keepdims=True))).astype(jnp.bfloat16)
        attn = jnp.einsum('hgij,jhd->ihgd', probs.astype(jnp.float32), value_expanded).astype(jnp.bfloat16)
        attn = attn.reshape(ROW_TOKENS, QUERY_HEADS * HEAD_SIZE)
        total = jnp.zeros((ROW_TOKENS, MODEL_WIDTH), jnp.float32)
        for group in range(N_MP):
            part = jnp.dot(attn[:, group * group_width:(group + 1) * group_width], o_weight[group * group_width:(group + 1) * group_width], preferred_element_type=jnp.float32).astype(jnp.bfloat16)
            part = lax.optimization_barrier(part)
            total = total + part.astype(jnp.float32)
        return total.astype(jnp.bfloat16)
    result = lax.map(one_row, (packed.reshape(ROWS, ROW_TOKENS, MODEL_WIDTH), block_ids.reshape(ROWS, ROW_TOKENS)))
    return result.reshape(TOKENS, MODEL_WIDTH)
```

```python
import functools

import jax
import jax.numpy as jnp
from jax import lax
from jax.experimental import pallas as pl
from jax.experimental.pallas import tpu as pltpu
from jax.sharding import Mesh, PartitionSpec as P

HEAD_SIZE = 128
ROW_TOKENS = 128
QUERY_PER_KV = 4
BF = jnp.bfloat16
F32 = jnp.float32

VMEM = pl.BlockSpec(memory_space=pltpu.VMEM)
SMEM = pl.BlockSpec(memory_space=pltpu.SMEM)
ANY = pl.BlockSpec(memory_space=pl.ANY)
CHUNKS = 2
STEPS = (0, 3, 1, 2)


def params(mib):
    return pltpu.CompilerParams(vmem_limit_bytes=mib * 1024 * 1024)


def cost(flops, nbytes):
    return pl.CostEstimate(flops=flops, bytes_accessed=nbytes, transcendentals=0)


def dispatch_kernel(rows_dev, place, pair_row, pairs, out):
    count, _, width = pairs.shape
    half = width // 2
    for p in range(count):
        owner = lax.div(pair_row[place[0] * count + p], rows_dev)
        chip = lax.div(owner, 2)
        core = owner - 2 * chip
        for k in range(2):
            out[chip, k, core] = pairs[p, :, k * half : (k + 1) * half]


def dispatch(own, pair_row, pair_tokens, rows_dev):
    count, cap, width = pair_tokens.shape
    return pl.pallas_call(
        functools.partial(dispatch_kernel, rows_dev),
        in_specs=[SMEM, SMEM, VMEM],
        out_specs=VMEM,
        out_shape=jax.ShapeDtypeStruct((count // 2, 2, 2, cap, width // 2), BF),
        name="dispatch",
        compiler_params=params(36),
        cost_estimate=cost(0, 4 * count * cap * width),
    )(own.reshape(1), pair_row, pair_tokens)


def pack_kernel(target, incoming, packed):
    sources, cores, cap, width = incoming.shape
    rows = packed.shape[0] // cores
    for core in range(cores):
        slots = incoming[:, core].reshape(sources * cap, width)
        wanted = lax.broadcasted_iota(jnp.int32, (rows, sources * cap), 0)
        pick = (wanted == target[core : core + 1, :]).astype(F32).astype(BF)
        wide = jnp.dot(pick, slots, preferred_element_type=F32)
        packed[pl.ds(core * rows, rows), :] = wide.astype(BF)


def pack(target, incoming, rows):
    sources, cores, cap, width = incoming.shape
    return pl.pallas_call(
        pack_kernel,
        in_specs=[VMEM] * 2,
        out_specs=VMEM,
        out_shape=jax.ShapeDtypeStruct((rows, width), BF),
        name="pack",
        compiler_params=params(36),
        cost_estimate=cost(2 * rows * sources * cap * width, 4 * sources * cap * width),
    )(target, incoming)


def stage_rows_kernel(place, source, out, sems):
    core = place[2]
    blocks, _, span, _ = out.shape
    copies = []
    for k in range(blocks):
        for owner in range(2):
            part = core if owner == 1 else 1 - core
            copies.append(
                pltpu.make_async_copy(
                    source.at[k, pl.ds(owner * span, span)], out.at[k, part], sems.at[k, owner]
                )
            )
    for copy in copies:
        copy.start()
    for copy in copies:
        copy.wait()


def stage_rows(place, source):
    blocks, tokens, depth = source.shape
    return pl.pallas_call(
        stage_rows_kernel,
        in_specs=[SMEM, ANY],
        out_specs=VMEM,
        out_shape=pltpu.VMEM((blocks, 2, tokens // 2, depth), BF),
        scratch_shapes=[pltpu.SemaphoreType.DMA((blocks, 2))],
        name="stage_rows",
        compiler_params=params(16),
        cost_estimate=cost(0, 4 * source.size),
    )(place, source)


def stage_kernel(*refs):
    sources, out, sems = refs[:-2], refs[-2], refs[-1]
    copies = [
        pltpu.make_async_copy(source, out.at[i], sems.at[i]) for i, source in enumerate(sources)
    ]
    for copy in copies:
        copy.start()
    for copy in copies:
        copy.wait()


def stage(sources):
    count = len(sources)
    return pl.pallas_call(
        stage_kernel,
        in_specs=[ANY] * count,
        out_specs=VMEM,
        out_shape=pltpu.VMEM((count, *sources[0].shape), BF),
        scratch_shapes=[pltpu.SemaphoreType.DMA((count,))],
        name="stage",
        compiler_params=params(16),
        cost_estimate=cost(0, 4 * count * sources[0].size),
    )(*sources)


def project_kernel(place, x, w_q, far_low, far_high, kv_first, kv_second, *refs):
    keeps, sends, squares = refs[:CHUNKS], refs[CHUNKS : 2 * CHUNKS], refs[2 * CHUNKS]
    y, first = place[1], place[3]
    rows = keeps[0].shape[1]
    span = rows * CHUNKS
    depth = x.shape[3]
    blocks = [lax.rem(y + step, 4) for step in STEPS]
    tile = 256
    wide = w_q.shape[3]
    for which in range(2):
        slot = first if which == 0 else 1 - first
        for begin in range(0, wide + kv_first.shape[2], tile):
            total = jnp.zeros((2 * span, tile), F32)
            for k in range(4):
                here = slice(begin, begin + tile)
                if begin >= wide:
                    piece = (kv_first, kv_second)[which][k, :, begin - wide : begin - wide + tile]
                elif k < 3:
                    piece = w_q[k, which, :, here]
                else:
                    piece = (far_low, far_high)[which][:, here]
                total += jnp.dot(
                    x[blocks[k]].reshape(2 * span, depth), piece, preferred_element_type=F32
                )
            for chunk in range(CHUNKS):
                lo = chunk * rows
                sends[chunk][slot, :, here] = total[lo : lo + rows].astype(BF)
                keeps[chunk][slot, :, here] = total[span + lo : span + lo + rows]
    for part in range(2):
        total = jnp.zeros((span, depth), F32)
        for k in range(4):
            wide = x[k, part].astype(F32)
            total += wide * wide
        squares[part] = jnp.sum(total, axis=1, keepdims=True)


def project(place, x, w_q, far_low, far_high, kv_first, kv_second):
    _, _, span, depth = x.shape
    columns = w_q.shape[3] + kv_first.shape[2]
    rows = span // CHUNKS
    results = pl.pallas_call(
        project_kernel,
        in_specs=[SMEM] + [VMEM] * 6,
        out_specs=[VMEM] * (2 * CHUNKS + 1),
        out_shape=[pltpu.VMEM((2, rows, columns), F32)] * CHUNKS
        + [jax.ShapeDtypeStruct((2, rows, columns), BF)] * CHUNKS
        + [jax.ShapeDtypeStruct((2, span, 1), F32)],
        name="project",
        compiler_params=params(24),
        cost_estimate=cost(4 * span * depth * 4 * columns * 2, 10 * 1024 * 1024),
    )(place, x, w_q, far_low, far_high, kv_first, kv_second)
    return results[:CHUNKS], results[CHUNKS : 2 * CHUNKS], results[2 * CHUNKS]


def attend_kernel(chunk, keep, *refs):
    sources, out, held, sems = refs[:5], refs[5], refs[6:11], refs[11]
    tokens = out.shape[0]
    rows = pl.ds(chunk * tokens, tokens)
    near, across, squares, turns, bias = sources
    parts = (near.at[0], across, squares.at[rows], turns.at[rows], bias.at[rows])
    copies = [
        pltpu.make_async_copy(part, place, sems.at[i])
        for i, (part, place) in enumerate(zip(parts, held))
    ]
    for copy in copies:
        copy.start()
    theirs, across, squares, turns, bias = held
    heads = out.shape[1] // HEAD_SIZE
    width = heads * HEAD_SIZE
    low = lax.broadcasted_iota(jnp.int32, (ROW_TOKENS, HEAD_SIZE), 1) < HEAD_SIZE // 2
    for copy in copies:
        copy.wait()
    for r in range(tokens // ROW_TOKENS):
        here = slice(r * ROW_TOKENS, (r + 1) * ROW_TOKENS)
        scale = lax.rsqrt(squares[here, :] + 1e-05)
        both = keep[0, here, :] + theirs[here, :].astype(F32) + across[here, :].astype(F32)
        both = both * scale
        turn = turns[here, :]
        turned = pltpu.roll(turn, HEAD_SIZE // 2, 1)
        cos = jnp.where(low, turn, turned)
        sin = jnp.where(low, -turned, turn)

        def rotate(u):
            return (u * cos + pltpu.roll(u, HEAD_SIZE // 2, 1) * sin).astype(BF)

        key = rotate(both[:, width : width + HEAD_SIZE])
        value = both[:, width + HEAD_SIZE :].astype(BF)
        query = jnp.concatenate(
            [rotate(both[:, h * HEAD_SIZE : (h + 1) * HEAD_SIZE]) for h in range(heads)], axis=0
        )
        scores = lax.dot_general(
            query, key, (((1,), (1,)), ((), ())), preferred_element_type=F32
        ) * HEAD_SIZE ** (-0.5)
        scores = scores + jnp.concatenate([bias[here, :]] * heads, axis=0)
        top = jnp.max(scores, axis=-1, keepdims=True)
        expo = jnp.exp(scores - top)
        probs = (expo / jnp.sum(expo, axis=-1, keepdims=True)).astype(BF)
        result = jnp.dot(probs, value, preferred_element_type=F32).astype(BF)
        for h in range(heads):
            out[here, h * HEAD_SIZE : (h + 1) * HEAD_SIZE] = result[
                h * ROW_TOKENS : (h + 1) * ROW_TOKENS
            ]


def attend(chunk, keep, near, across, squares, turns, bias):
    _, tokens, columns = keep.shape
    width = columns - 2 * HEAD_SIZE
    return pl.pallas_call(
        functools.partial(attend_kernel, chunk),
        in_specs=[VMEM] + [pl.BlockSpec(memory_space=pltpu.HBM)] * 5,
        out_specs=VMEM,
        out_shape=jax.ShapeDtypeStruct((tokens, width), BF),
        scratch_shapes=[
            pltpu.VMEM((tokens, columns), BF),
            pltpu.VMEM((tokens, columns), BF),
            pltpu.VMEM((tokens, 1), F32),
            pltpu.VMEM((tokens, HEAD_SIZE), F32),
            pltpu.VMEM((tokens, ROW_TOKENS), F32),
            pltpu.SemaphoreType.DMA((5,)),
        ],
        name="attend",
        compiler_params=params(16),
        cost_estimate=cost(4 * tokens * width * ROW_TOKENS, 8 * tokens * columns),
    )(keep, near, across, squares, turns, bias)


def expand_kernel(steps, place, mine, other, weights, *outs):
    z, first = place[0], place[3]
    straight = first == 0
    left = jnp.where(straight, mine[...], other[...])
    right = jnp.where(straight, other[...], mine[...])
    rows = outs[0].shape[0]
    wide = weights.shape[-1]
    for i, step in enumerate(steps):
        block = 2 * lax.rem(z + step, 4)
        for k in range(2):
            total = jnp.dot(left, weights[block + k, 0], preferred_element_type=F32)
            total += jnp.dot(right, weights[block + k, 1], preferred_element_type=F32)
            total = total.astype(BF)
            outs[2 * i][:, k * wide : (k + 1) * wide] = total[:rows]
            outs[2 * i + 1][:, k * wide : (k + 1) * wide] = total[rows:]


def expand(steps, place, mine, other, weights):
    tokens, depth = mine.shape
    wide = weights.shape[-1]
    count = len(steps)
    return pl.pallas_call(
        functools.partial(expand_kernel, steps),
        in_specs=[SMEM, VMEM, VMEM, VMEM],
        out_specs=[VMEM] * (2 * count),
        out_shape=[jax.ShapeDtypeStruct((tokens // 2, 2 * wide), BF)] * (2 * count),
        name="expand",
        compiler_params=params(16),
        cost_estimate=cost(count * 8 * tokens * depth * wide, count * 3 * 1024 * 1024),
    )(place, mine, other, weights)


def after(values, *events):
    return lax.optimization_barrier((*values, *events))


def shift(x, axis, by):
    size = lax.axis_size(axis)
    return lax.ppermute(x, axis, [(i, (i + by) % size) for i in range(size)])


def spread(x):
    def at(place):
        return (place % 2) * 2 + place // 2

    first = [(0, 1), (1, 3), (2, 0), (3, 2)]
    second = [(0, 0), (1, 2), (2, 1), (3, 3)]
    return tuple(
        lax.ppermute(x, ("xl", "xh"), [(at(a), at(b)) for a, b in pairs])
        for pairs in (first, second)
    )


def row_mask(ids):
    pair_of = ids // 3
    role_of = ids % 3
    steps_a = jnp.arange(ids.shape[0])
    causal = steps_a[None, :] <= steps_a[:, None]
    same = pair_of[:, None] == pair_of[None, :]
    hidden_pair = (role_of[:, None] == 2) & (role_of[None, :] == 1)
    return causal & same & jnp.logical_not(hidden_pair)


def local(
    pair_tokens,
    norm_gain,
    q_weight,
    k_weight,
    value_weight,
    o_weight,
    pair_row,
    pair_span,
    block_ids,
):
    dp = ("xl", "y", "c")
    dp_count = lax.axis_size(dp)
    own = lax.axis_index(dp)
    xl, y, core = (lax.axis_index(a) for a in dp)
    xh, z = lax.axis_index("xh"), lax.axis_index("z")
    pairs_dev, pair_cap, width_local = pair_tokens.shape
    tok_dev = block_ids.shape[0]
    rows_dev = tok_dev // ROW_TOKENS
    first = jnp.where(xh == 1 - xl, 0, 1).astype(jnp.int32)

    owners_all = (pair_row // rows_dev).reshape(dp_count, pairs_dev)
    rows = q_weight.shape[0]
    gain = lax.dynamic_slice_in_dim(norm_gain, own * rows, rows, 0)[:, None]
    q_in = (q_weight.astype(F32) * gain).astype(BF)
    kv_in = jnp.concatenate([k_weight, value_weight], axis=1)
    kv_in = (kv_in.astype(F32) * gain).astype(BF)
    outgoing = dispatch(own.astype(jnp.int32), pair_row, pair_tokens, rows_dev)
    q_pair = spread(q_in)
    kv_blocks = (kv_in, shift(kv_in, "y", 1), shift(kv_in, "y", -1), shift(kv_in, "y", 2))
    outgoing = outgoing.reshape(dp_count, 2, pair_cap, width_local // 2)
    incoming = lax.all_to_all(outgoing, dp, split_axis=0, concat_axis=0, tiled=True)

    incoming = after((incoming,), *q_pair, *kv_blocks)[0]

    slots = jnp.arange(pair_cap, dtype=jnp.int32)
    begin = ((pair_row % rows_dev) * ROW_TOKENS + pair_span[:, 0]).reshape(dp_count, pairs_dev)
    length = (pair_span[:, 1] - pair_span[:, 0]).reshape(dp_count, pairs_dev)
    owner_here = (own // 2) * 2 + jnp.arange(2, dtype=jnp.int32)
    match = owners_all[None] == owner_here[:, None, None]
    begin_here = jnp.sum(jnp.where(match, begin[None], 0), axis=2)
    length_here = jnp.sum(jnp.where(match, length[None], 0), axis=2)
    target = jnp.where(
        slots[None, None, :] < length_here[:, :, None],
        begin_here[:, :, None] + slots[None, None, :],
        -1,
    ).reshape(2, dp_count * pair_cap)
    packed = pack(target, incoming, 2 * tok_dev)
    x_blocks = lax.all_gather(packed, "z", axis=0, tiled=False)

    q_both = jnp.stack(after(q_pair, packed)[:2])
    q_before, q_behind = shift(q_both, "y", 1), shift(q_both, "y", -1)
    kv_all = jnp.stack(after(kv_blocks, packed)[:4])
    kv_first, kv_second = spread(kv_all)
    q_from, q_back = after((q_before, q_behind), kv_first, kv_second)[:2]
    far_low, far_high = shift(q_from[0], "y", 1), shift(q_back[1], "y", -1)
    w_q = stage((q_both, q_before, q_behind))

    o_in = after((o_weight,), q_before, q_behind, kv_first, kv_second)[0]
    o_both = after((jnp.stack(spread(o_in)),), x_blocks)[0]
    o_all = lax.all_gather(o_both, ("y", "c"), axis=0, tiled=False)

    place = jnp.stack([z, y, core, first]).astype(jnp.int32)
    x_all = stage_rows(place, x_blocks)
    visible = jax.vmap(row_mask)(block_ids.reshape(rows_dev, ROW_TOKENS))
    position = (jnp.sum(visible.astype(jnp.int32), axis=2) - 1).reshape(tok_dev)
    half = HEAD_SIZE // 2
    freq = 500000.0 ** (-(jnp.arange(half, dtype=F32) * 2.0 / HEAD_SIZE))
    angle = position.astype(F32)[:, None] * freq[None, :]
    turns = jnp.concatenate([jnp.cos(angle), jnp.sin(angle)], axis=1)

    bias = jnp.where(visible, 0.0, -1e30).astype(F32).reshape(tok_dev, ROW_TOKENS)

    place, turns, bias, x_all, w_q = lax.optimization_barrier((place, turns, bias, x_all, w_q))

    outputs = []
    keeps, sends, squares = project(place, x_all, w_q, far_low, far_high, kv_first, kv_second)
    squares = squares.reshape(2, tok_dev // 128, 128)
    squares = squares[1] + shift(squares[0], "c", 1)
    squares = squares + shift(squares, "xh", 1)
    mean = squares.reshape(tok_dev, 1) * (1.0 / norm_gain.shape[0])
    for chunk in range(CHUNKS):
        keep, send = keeps[chunk], sends[chunk]
        near = shift(send, "c", 1)
        across = shift((keep[1] + near[1].astype(F32)).astype(BF), "xh", 1)
        attn = attend(chunk, keep, near, across, mean, turns, bias)
        attn_other = shift(attn, "xh", 1)
        far_low, far_high = expand((2,), place, attn, attn_other, o_all)
        from_before = shift(far_low, "z", 1)
        from_behind = shift(far_high, "z", -1)
        up_low, up_high, down_low, down_high, low, high = expand(
            (1, 3, 0), place, attn, attn_other, o_all
        )
        up_high = shift(up_high, "z", 1)
        down_low = shift(down_low, "z", -1)
        up_low = shift((up_low.astype(F32) + from_before.astype(F32)).astype(BF), "z", 1)
        down_high = shift((down_high.astype(F32) + from_behind.astype(F32)).astype(BF), "z", -1)
        low = low.astype(F32) + up_low.astype(F32) + down_low.astype(F32)
        high = high.astype(F32) + up_high.astype(F32) + down_high.astype(F32)
        outputs += [low.astype(BF), high.astype(BF)]
    return jnp.concatenate(outputs, axis=0)


def solution(mesh):
    fine = Mesh(mesh.devices.reshape(2, 4, 2, 2, 4), ("xl", "y", "c", "xh", "z"))
    dp, mp = ("xl", "y", "c"), ("xh", "z")
    placed = (
        P(dp, None, mp),
        P(),
        P(dp, mp),
        P(dp, mp),
        P(dp, mp),
        P(mp, dp),
        P(),
        P(),
        P(dp),
    )
    return jax.shard_map(
        local, mesh=fine, in_specs=placed, out_specs=P(dp, mp), check_vma=False
    )
```

```python
import functools

import jax
import jax.numpy as jnp
from jax import lax
from jax.experimental import pallas as pl
from jax.experimental.pallas import tpu as pltpu
from jax.sharding import Mesh, PartitionSpec as P

HEAD_SIZE = 128
ROW_TOKENS = 128
QUERY_PER_KV = 4
BF = jnp.bfloat16
F32 = jnp.float32

VMEM = pl.BlockSpec(memory_space=pltpu.VMEM)
SMEM = pl.BlockSpec(memory_space=pltpu.SMEM)
ANY = pl.BlockSpec(memory_space=pl.ANY)
CHUNKS = 2
STEPS = (0, 3, 1, 2)


def params(mib):
    return pltpu.CompilerParams(vmem_limit_bytes=mib * 1024 * 1024)


def cost(flops, nbytes):
    return pl.CostEstimate(flops=flops, bytes_accessed=nbytes, transcendentals=0)


def dispatch_kernel(rows_dev, place, pair_row, pairs, out):
    count, _, width = pairs.shape
    half = width // 2
    for p in range(count):
        owner = lax.div(pair_row[place[0] * count + p], rows_dev)
        chip = lax.div(owner, 2)
        core = owner - 2 * chip
        for k in range(2):
            out[chip, k, core] = pairs[p, :, k * half : (k + 1) * half]


def dispatch(own, pair_row, pair_tokens, rows_dev):
    count, cap, width = pair_tokens.shape
    return pl.pallas_call(
        functools.partial(dispatch_kernel, rows_dev),
        in_specs=[SMEM, SMEM, VMEM],
        out_specs=VMEM,
        out_shape=jax.ShapeDtypeStruct((count // 2, 2, 2, cap, width // 2), BF),
        name="dispatch",
        compiler_params=params(36),
        cost_estimate=cost(0, 4 * count * cap * width),
    )(own.reshape(1), pair_row, pair_tokens)


def pack_kernel(target, incoming, packed):
    sources, cores, cap, width = incoming.shape
    rows = packed.shape[0] // cores
    for core in range(cores):
        slots = incoming[:, core].reshape(sources * cap, width)
        wanted = lax.broadcasted_iota(jnp.int32, (rows, sources * cap), 0)
        pick = (wanted == target[core : core + 1, :]).astype(F32).astype(BF)
        wide = jnp.dot(pick, slots, preferred_element_type=F32)
        packed[pl.ds(core * rows, rows), :] = wide.astype(BF)


def pack(target, incoming, rows):
    sources, cores, cap, width = incoming.shape
    return pl.pallas_call(
        pack_kernel,
        in_specs=[VMEM] * 2,
        out_specs=VMEM,
        out_shape=jax.ShapeDtypeStruct((rows, width), BF),
        name="pack",
        compiler_params=params(36),
        cost_estimate=cost(2 * rows * sources * cap * width, 4 * sources * cap * width),
    )(target, incoming)


def stage_rows_kernel(place, source, out, sems):
    core = place[2]
    blocks, _, span, _ = out.shape
    copies = []
    for k in range(blocks):
        for owner in range(2):
            part = core if owner == 1 else 1 - core
            copies.append(
                pltpu.make_async_copy(
                    source.at[k, pl.ds(owner * span, span)], out.at[k, part], sems.at[k, owner]
                )
            )
    for copy in copies:
        copy.start()
    for copy in copies:
        copy.wait()


def stage_rows(place, source):
    blocks, tokens, depth = source.shape
    return pl.pallas_call(
        stage_rows_kernel,
        in_specs=[SMEM, ANY],
        out_specs=VMEM,
        out_shape=pltpu.VMEM((blocks, 2, tokens // 2, depth), BF),
        scratch_shapes=[pltpu.SemaphoreType.DMA((blocks, 2))],
        name="stage_rows",
        compiler_params=params(16),
        cost_estimate=cost(0, 4 * source.size),
    )(place, source)


def stage_kernel(*refs):
    sources, out, sems = refs[:-2], refs[-2], refs[-1]
    copies = [
        pltpu.make_async_copy(source, out.at[i], sems.at[i]) for i, source in enumerate(sources)
    ]
    for copy in copies:
        copy.start()
    for copy in copies:
        copy.wait()


def stage(sources):
    count = len(sources)
    return pl.pallas_call(
        stage_kernel,
        in_specs=[ANY] * count,
        out_specs=VMEM,
        out_shape=pltpu.VMEM((count, *sources[0].shape), BF),
        scratch_shapes=[pltpu.SemaphoreType.DMA((count,))],
        name="stage",
        compiler_params=params(16),
        cost_estimate=cost(0, 4 * count * sources[0].size),
    )(*sources)


def project_kernel(place, x, w_q, far_low, far_high, kv_first, kv_second, *refs):
    keeps, sends, squares = refs[:CHUNKS], refs[CHUNKS : 2 * CHUNKS], refs[2 * CHUNKS]
    y, first = place[1], place[3]
    rows = keeps[0].shape[1]
    span = rows * CHUNKS
    depth = x.shape[3]
    blocks = [lax.rem(y + step, 4) for step in STEPS]
    tile = 256
    wide = w_q.shape[3]
    for which in range(2):
        slot = first if which == 0 else 1 - first
        for begin in range(0, wide + kv_first.shape[2], tile):
            total = jnp.zeros((2 * span, tile), F32)
            for k in range(4):
                here = slice(begin, begin + tile)
                if begin >= wide:
                    piece = (kv_first, kv_second)[which][k, :, begin - wide : begin - wide + tile]
                elif k < 3:
                    piece = w_q[k, which, :, here]
                else:
                    piece = (far_low, far_high)[which][:, here]
                total += jnp.dot(
                    x[blocks[k]].reshape(2 * span, depth), piece, preferred_element_type=F32
                )
            for chunk in range(CHUNKS):
                lo = chunk * rows
                sends[chunk][slot, :, here] = total[lo : lo + rows].astype(BF)
                keeps[chunk][slot, :, here] = total[span + lo : span + lo + rows]
    for part in range(2):
        total = jnp.zeros((span, depth), F32)
        for k in range(4):
            wide = x[k, part].astype(F32)
            total += wide * wide
        squares[part] = jnp.sum(total, axis=1, keepdims=True)


def project(place, x, w_q, far_low, far_high, kv_first, kv_second):
    _, _, span, depth = x.shape
    columns = w_q.shape[3] + kv_first.shape[2]
    rows = span // CHUNKS
    results = pl.pallas_call(
        project_kernel,
        in_specs=[SMEM] + [VMEM] * 6,
        out_specs=[VMEM] * (2 * CHUNKS + 1),
        out_shape=[pltpu.VMEM((2, rows, columns), F32)] * CHUNKS
        + [jax.ShapeDtypeStruct((2, rows, columns), BF)] * CHUNKS
        + [jax.ShapeDtypeStruct((2, span, 1), F32)],
        name="project",
        compiler_params=params(24),
        cost_estimate=cost(4 * span * depth * 4 * columns * 2, 10 * 1024 * 1024),
    )(place, x, w_q, far_low, far_high, kv_first, kv_second)
    return results[:CHUNKS], results[CHUNKS : 2 * CHUNKS], results[2 * CHUNKS]


def tables_kernel(turns, bias, out):
    out[0] = turns[...]
    out[1] = bias[...]


def tables(turns, bias):
    return pl.pallas_call(
        tables_kernel,
        in_specs=[VMEM] * 2,
        out_specs=VMEM,
        out_shape=pltpu.VMEM((2, *turns.shape), F32),
        name="tables",
        compiler_params=params(16),
        cost_estimate=cost(0, 16 * turns.size),
    )(turns, bias)


def attend_kernel(chunk, keep, near, across, squares, table, out):
    tokens = out.shape[0]
    heads = out.shape[1] // HEAD_SIZE
    width = heads * HEAD_SIZE
    lane = lax.broadcasted_iota(jnp.int32, (ROW_TOKENS, HEAD_SIZE), 1)
    low = lane < HEAD_SIZE // 2
    diagonal = lane == lax.broadcasted_iota(jnp.int32, (ROW_TOKENS, HEAD_SIZE), 0)
    for r in range(tokens // ROW_TOKENS):
        here = slice(r * ROW_TOKENS, (r + 1) * ROW_TOKENS)
        row = chunk * (tokens // ROW_TOKENS) + r
        there = slice(row * ROW_TOKENS, (row + 1) * ROW_TOKENS)
        column = jnp.sum(jnp.where(diagonal, squares[row : row + 1, :], 0.0), axis=1, keepdims=True)
        scale = lax.rsqrt(column + 1e-05)
        both = keep[0, here, :] + near[0, here, :].astype(F32) + across[here, :].astype(F32)
        both = both * scale
        turn = table[0, there, :]
        turned = pltpu.roll(turn, HEAD_SIZE // 2, 1)
        cos = jnp.where(low, turn, turned)
        sin = jnp.where(low, -turned, turn)

        def rotate(u):
            return (u * cos + pltpu.roll(u, HEAD_SIZE // 2, 1) * sin).astype(BF)

        key = rotate(both[:, width : width + HEAD_SIZE])
        value = both[:, width + HEAD_SIZE :].astype(BF)
        query = jnp.concatenate(
            [rotate(both[:, h * HEAD_SIZE : (h + 1) * HEAD_SIZE]) for h in range(heads)], axis=0
        )
        scores = lax.dot_general(
            query, key, (((1,), (1,)), ((), ())), preferred_element_type=F32
        ) * HEAD_SIZE ** (-0.5)
        scores = scores + jnp.concatenate([table[1, there, :]] * heads, axis=0)
        top = jnp.max(scores, axis=-1, keepdims=True)
        expo = jnp.exp(scores - top)
        probs = (expo / jnp.sum(expo, axis=-1, keepdims=True)).astype(BF)
        result = jnp.dot(probs, value, preferred_element_type=F32).astype(BF)
        for h in range(heads):
            out[here, h * HEAD_SIZE : (h + 1) * HEAD_SIZE] = result[
                h * ROW_TOKENS : (h + 1) * ROW_TOKENS
            ]


def attend(chunk, keep, near, across, squares, table):
    _, tokens, columns = keep.shape
    width = columns - 2 * HEAD_SIZE
    return pl.pallas_call(
        functools.partial(attend_kernel, chunk),
        in_specs=[VMEM] * 5,
        out_specs=VMEM,
        out_shape=jax.ShapeDtypeStruct((tokens, width), BF),
        name="attend",
        compiler_params=params(16),
        cost_estimate=cost(4 * tokens * width * ROW_TOKENS, 8 * tokens * columns),
    )(keep, near, across, squares, table)


def expand_kernel(steps, place, mine, other, weights, *outs):
    z, first = place[0], place[3]
    straight = first == 0
    left = jnp.where(straight, mine[...], other[...])
    right = jnp.where(straight, other[...], mine[...])
    wide = weights.shape[-1]
    for out, step in zip(outs, steps):
        block = 2 * lax.rem(z + step, 4)
        for k in range(2):
            total = jnp.dot(left, weights[block + k, 0], preferred_element_type=F32)
            total += jnp.dot(right, weights[block + k, 1], preferred_element_type=F32)
            out[:, k * wide : (k + 1) * wide] = total.astype(BF)


def expand(steps, place, mine, other, weights):
    tokens, depth = mine.shape
    wide = weights.shape[-1]
    count = len(steps)
    return pl.pallas_call(
        functools.partial(expand_kernel, steps),
        in_specs=[SMEM, VMEM, VMEM, VMEM],
        out_specs=[VMEM] * count,
        out_shape=[jax.ShapeDtypeStruct((tokens, 2 * wide), BF)] * count,
        name="expand",
        compiler_params=params(16),
        cost_estimate=cost(count * 8 * tokens * depth * wide, count * 3 * 1024 * 1024),
    )(place, mine, other, weights)


def after(values, *events):
    return lax.optimization_barrier((*values, *events))


def shift(x, axis, by):
    size = lax.axis_size(axis)
    return lax.ppermute(x, axis, [(i, (i + by) % size) for i in range(size)])


def spread(x):
    def at(place):
        return (place % 2) * 2 + place // 2

    first = [(0, 1), (1, 3), (2, 0), (3, 2)]
    second = [(0, 0), (1, 2), (2, 1), (3, 3)]
    return tuple(
        lax.ppermute(x, ("xl", "xh"), [(at(a), at(b)) for a, b in pairs])
        for pairs in (first, second)
    )


def row_mask(ids):
    pair_of = ids // 3
    role_of = ids % 3
    steps_a = jnp.arange(ids.shape[0])
    causal = steps_a[None, :] <= steps_a[:, None]
    same = pair_of[:, None] == pair_of[None, :]
    hidden_pair = (role_of[:, None] == 2) & (role_of[None, :] == 1)
    return causal & same & jnp.logical_not(hidden_pair)


def local(
    pair_tokens,
    norm_gain,
    q_weight,
    k_weight,
    value_weight,
    o_weight,
    pair_row,
    pair_span,
    block_ids,
):
    dp = ("xl", "y", "c")
    dp_count = lax.axis_size(dp)
    own = lax.axis_index(dp)
    xl, y, core = (lax.axis_index(a) for a in dp)
    xh, z = lax.axis_index("xh"), lax.axis_index("z")
    pairs_dev, pair_cap, width_local = pair_tokens.shape
    tok_dev = block_ids.shape[0]
    rows_dev = tok_dev // ROW_TOKENS
    first = jnp.where(xh == 1 - xl, 0, 1).astype(jnp.int32)

    owners_all = (pair_row // rows_dev).reshape(dp_count, pairs_dev)
    rows = q_weight.shape[0]
    gain = lax.dynamic_slice_in_dim(norm_gain, own * rows, rows, 0)[:, None]
    q_in = (q_weight.astype(F32) * gain).astype(BF)
    kv_in = jnp.concatenate([k_weight, value_weight], axis=1)
    kv_in = (kv_in.astype(F32) * gain).astype(BF)
    outgoing = dispatch(own.astype(jnp.int32), pair_row, pair_tokens, rows_dev)
    q_pair = spread(q_in)
    kv_blocks = (kv_in, shift(kv_in, "y", 1), shift(kv_in, "y", -1), shift(kv_in, "y", 2))
    outgoing = outgoing.reshape(dp_count, 2, pair_cap, width_local // 2)
    incoming = lax.all_to_all(outgoing, dp, split_axis=0, concat_axis=0, tiled=True)

    incoming = after((incoming,), *q_pair, *kv_blocks)[0]

    slots = jnp.arange(pair_cap, dtype=jnp.int32)
    begin = ((pair_row % rows_dev) * ROW_TOKENS + pair_span[:, 0]).reshape(dp_count, pairs_dev)
    length = (pair_span[:, 1] - pair_span[:, 0]).reshape(dp_count, pairs_dev)
    owner_here = (own // 2) * 2 + jnp.arange(2, dtype=jnp.int32)
    match = owners_all[None] == owner_here[:, None, None]
    begin_here = jnp.sum(jnp.where(match, begin[None], 0), axis=2)
    length_here = jnp.sum(jnp.where(match, length[None], 0), axis=2)
    target = jnp.where(
        slots[None, None, :] < length_here[:, :, None],
        begin_here[:, :, None] + slots[None, None, :],
        -1,
    ).reshape(2, dp_count * pair_cap)
    packed = pack(target, incoming, 2 * tok_dev)
    x_blocks = lax.all_gather(packed, "z", axis=0, tiled=False)

    q_both = jnp.stack(after(q_pair, packed)[:2])
    q_before, q_behind = shift(q_both, "y", 1), shift(q_both, "y", -1)
    kv_all = jnp.stack(after(kv_blocks, packed)[:4])
    kv_first, kv_second = spread(kv_all)
    q_from, q_back = after((q_before, q_behind), kv_first, kv_second)[:2]
    far_low, far_high = shift(q_from[0], "y", 1), shift(q_back[1], "y", -1)
    w_q = stage((q_both, q_before, q_behind))

    visible = jax.vmap(row_mask)(block_ids.reshape(rows_dev, ROW_TOKENS))
    position = (jnp.sum(visible.astype(jnp.int32), axis=2) - 1).reshape(tok_dev)
    half = HEAD_SIZE // 2
    freq = 500000.0 ** (-(jnp.arange(half, dtype=F32) * 2.0 / HEAD_SIZE))
    angle = position.astype(F32)[:, None] * freq[None, :]
    turns = jnp.concatenate([jnp.cos(angle), jnp.sin(angle)], axis=1)

    bias = jnp.where(visible, 0.0, -1e30).astype(F32).reshape(tok_dev, ROW_TOKENS)

    table = tables(turns, bias)

    o_in = after((o_weight,), q_from, q_back, table)[0]
    o_pair = after(spread(o_in), far_low, far_high)[:2]
    o_both = after((jnp.stack(o_pair),), x_blocks)[0]
    o_all = lax.all_gather(o_both, ("y", "c"), axis=0, tiled=False)

    place = jnp.stack([z, y, core, first]).astype(jnp.int32)
    x_all = stage_rows(place, x_blocks)
    place, table, x_all, w_q = lax.optimization_barrier((place, table, x_all, w_q))

    keeps, sends, squares = project(place, x_all, w_q, far_low, far_high, kv_first, kv_second)
    nears = [shift(send, "c", 1) for send in sends]
    others = [(keep[1] + near[1].astype(F32)).astype(BF) for keep, near in zip(keeps, nears)]
    acrosses = [shift(other, "xh", 1) for other in others]
    squares = after((squares.reshape(2, tok_dev // 128, 128),), others[0])[0]
    squares = squares[1] + shift(squares[0], "c", 1)
    squares = squares + shift(squares, "xh", 1)
    mean = squares * (1.0 / norm_gain.shape[0])
    attns = [
        attend(chunk, keeps[chunk], nears[chunk], acrosses[chunk], mean, table)
        for chunk in range(CHUNKS)
    ]
    swapped = [shift(attn, "xh", 1) for attn in attns]
    o_all = after((o_all,), *swapped)[0]

    def terms(chunk, steps):
        return expand(steps, place, attns[chunk], swapped[chunk], o_all)

    (far_low,) = terms(0, (2,))
    passing_low = shift(far_low, "z", 1)
    down_low, up_low, own_low = terms(0, (3, 1, 0))
    down_low = shift(down_low, "z", -1)
    (far_high,) = terms(1, (2,))
    passing_high = shift(far_high, "z", -1)
    up_high, down_high, own_high = terms(1, (1, 3, 0))
    up_high = shift(up_high, "z", 1)
    up_low = shift((up_low.astype(F32) + passing_low.astype(F32)).astype(BF), "z", 1)
    down_high = shift((down_high.astype(F32) + passing_high.astype(F32)).astype(BF), "z", -1)
    low = own_low.astype(F32) + up_low.astype(F32) + down_low.astype(F32)
    high = own_high.astype(F32) + up_high.astype(F32) + down_high.astype(F32)
    return jnp.concatenate([low.astype(BF), high.astype(BF)], axis=0)


def solution(mesh):
    fine = Mesh(mesh.devices.reshape(2, 4, 2, 2, 4), ("xl", "y", "c", "xh", "z"))
    dp, mp = ("xl", "y", "c"), ("xh", "z")
    placed = (
        P(dp, None, mp),
        P(),
        P(dp, mp),
        P(dp, mp),
        P(dp, mp),
        P(mp, dp),
        P(),
        P(),
        P(dp),
    )
    return jax.shard_map(
        local, mesh=fine, in_specs=placed, out_specs=P(dp, mp), check_vma=False
    )
```

```python
import functools

import jax
import jax.numpy as jnp
from jax import lax
from jax.experimental import pallas as pl
from jax.experimental.pallas import tpu as pltpu
from jax.sharding import Mesh, PartitionSpec as P

HEAD_SIZE = 128
ROW_TOKENS = 128
QUERY_PER_KV = 4
BF = jnp.bfloat16
F32 = jnp.float32

VMEM = pl.BlockSpec(memory_space=pltpu.VMEM)
SMEM = pl.BlockSpec(memory_space=pltpu.SMEM)
ANY = pl.BlockSpec(memory_space=pl.ANY)
CHUNKS = 2
STEPS = (0, 3, 1, 2)


def params(mib):
    return pltpu.CompilerParams(vmem_limit_bytes=mib * 1024 * 1024)


def cost(flops, nbytes):
    return pl.CostEstimate(flops=flops, bytes_accessed=nbytes, transcendentals=0)


def dispatch_kernel(rows_dev, place, pair_row, pairs, out):
    count, _, width = pairs.shape
    half = width // 2
    for p in range(count):
        owner = lax.div(pair_row[place[0] * count + p], rows_dev)
        chip = lax.div(owner, 2)
        core = owner - 2 * chip
        for k in range(2):
            out[chip, k, core] = pairs[p, :, k * half : (k + 1) * half]


def dispatch(own, pair_row, pair_tokens, rows_dev):
    count, cap, width = pair_tokens.shape
    return pl.pallas_call(
        functools.partial(dispatch_kernel, rows_dev),
        in_specs=[SMEM, SMEM, VMEM],
        out_specs=VMEM,
        out_shape=jax.ShapeDtypeStruct((count // 2, 2, 2, cap, width // 2), BF),
        name="dispatch",
        compiler_params=params(60),
        cost_estimate=cost(0, 4 * count * cap * width),
    )(own.reshape(1), pair_row, pair_tokens)


def pack_kernel(target, incoming, packed):
    sources, cores, cap, width = incoming.shape
    rows = packed.shape[0] // cores
    for core in range(cores):
        slots = incoming[:, core].reshape(sources * cap, width)
        wanted = lax.broadcasted_iota(jnp.int32, (rows, sources * cap), 0)
        pick = (wanted == target[core : core + 1, :]).astype(F32).astype(BF)
        wide = jnp.dot(pick, slots, preferred_element_type=F32)
        packed[pl.ds(core * rows, rows), :] = wide.astype(BF)


def pack(target, incoming, rows):
    sources, cores, cap, width = incoming.shape
    return pl.pallas_call(
        pack_kernel,
        in_specs=[VMEM] * 2,
        out_specs=VMEM,
        out_shape=jax.ShapeDtypeStruct((rows, width), BF),
        name="pack",
        compiler_params=params(36),
        cost_estimate=cost(2 * rows * sources * cap * width, 4 * sources * cap * width),
    )(target, incoming)


def stage_kernel(*refs):
    sources, out, sems = refs[:-2], refs[-2], refs[-1]
    copies = [
        pltpu.make_async_copy(source, out.at[i], sems.at[i]) for i, source in enumerate(sources)
    ]
    for copy in copies:
        copy.start()
    for copy in copies:
        copy.wait()


def stage(sources):
    count = len(sources)
    return pl.pallas_call(
        stage_kernel,
        in_specs=[ANY] * count,
        out_specs=VMEM,
        out_shape=pltpu.VMEM((count, *sources[0].shape), BF),
        scratch_shapes=[pltpu.SemaphoreType.DMA((count,))],
        name="stage",
        compiler_params=params(16),
        cost_estimate=cost(0, 4 * count * sources[0].size),
    )(*sources)


def project_kernel(place, x, w_q, far_low, far_high, kv_first, kv_second, *refs):
    keeps, sends, squares = refs[:CHUNKS], refs[CHUNKS : 2 * CHUNKS], refs[2 * CHUNKS]
    y, core, first = place[1], place[2], place[3]
    rows = keeps[0].shape[1]
    span = rows * CHUNKS
    depth = x.shape[2]

    def split(value):
        low, high = value[:span], value[span:]
        return jnp.where(core == 0, high, low), jnp.where(core == 0, low, high)

    blocks = [lax.rem(y + step, 4) for step in STEPS]
    tile = 256
    wide = w_q.shape[3]
    for which in range(2):
        slot = first if which == 0 else 1 - first
        for begin in range(0, wide + kv_first.shape[2], tile):
            total = jnp.zeros((2 * span, tile), F32)
            for k in range(4):
                here = slice(begin, begin + tile)
                if begin >= wide:
                    piece = (kv_first, kv_second)[which][k, :, begin - wide : begin - wide + tile]
                elif k < 3:
                    piece = w_q[k, which, :, here]
                else:
                    piece = (far_low, far_high)[which][:, here]
                total += jnp.dot(x[blocks[k]], piece, preferred_element_type=F32)
            theirs, mine = split(total)
            for chunk in range(CHUNKS):
                lo = chunk * rows
                sends[chunk][slot, :, here] = theirs[lo : lo + rows].astype(BF)
                keeps[chunk][slot, :, here] = mine[lo : lo + rows]
    total = jnp.zeros((2 * span, depth), F32)
    for k in range(4):
        wide = x[k].astype(F32)
        total += wide * wide
    squares[0], squares[1] = split(jnp.sum(total, axis=1, keepdims=True))


def project(place, x, w_q, far_low, far_high, kv_first, kv_second):
    _, tokens, depth = x.shape
    span = tokens // 2
    columns = w_q.shape[3] + kv_first.shape[2]
    rows = span // CHUNKS
    results = pl.pallas_call(
        project_kernel,
        in_specs=[SMEM] + [VMEM] * 6,
        out_specs=[VMEM] * (2 * CHUNKS + 1),
        out_shape=[pltpu.VMEM((2, rows, columns), F32)] * CHUNKS
        + [jax.ShapeDtypeStruct((2, rows, columns), BF)] * CHUNKS
        + [jax.ShapeDtypeStruct((2, span, 1), F32)],
        name="project",
        compiler_params=params(24),
        cost_estimate=cost(4 * span * depth * 4 * columns * 2, 10 * 1024 * 1024),
    )(place, x, w_q, far_low, far_high, kv_first, kv_second)
    return results[:CHUNKS], results[CHUNKS : 2 * CHUNKS], results[2 * CHUNKS]


def tables_kernel(turns, bias, out):
    out[0] = turns[...]
    out[1] = bias[...]


def tables(turns, bias):
    return pl.pallas_call(
        tables_kernel,
        in_specs=[VMEM] * 2,
        out_specs=VMEM,
        out_shape=pltpu.VMEM((2, *turns.shape), F32),
        name="tables",
        compiler_params=params(16),
        cost_estimate=cost(0, 16 * turns.size),
    )(turns, bias)


def attend_kernel(chunk, keep, near, across, squares, table, out):
    tokens = out.shape[0]
    heads = out.shape[1] // HEAD_SIZE
    width = heads * HEAD_SIZE
    lane = lax.broadcasted_iota(jnp.int32, (ROW_TOKENS, HEAD_SIZE), 1)
    low = lane < HEAD_SIZE // 2
    diagonal = lane == lax.broadcasted_iota(jnp.int32, (ROW_TOKENS, HEAD_SIZE), 0)
    for r in range(tokens // ROW_TOKENS):
        here = slice(r * ROW_TOKENS, (r + 1) * ROW_TOKENS)
        row = chunk * (tokens // ROW_TOKENS) + r
        there = slice(row * ROW_TOKENS, (row + 1) * ROW_TOKENS)
        column = jnp.sum(jnp.where(diagonal, squares[row : row + 1, :], 0.0), axis=1, keepdims=True)
        scale = lax.rsqrt(column + 1e-05)
        both = keep[0, here, :] + near[0, here, :].astype(F32) + across[here, :].astype(F32)
        both = both * scale
        turn = table[0, there, :]
        turned = pltpu.roll(turn, HEAD_SIZE // 2, 1)
        cos = jnp.where(low, turn, turned)
        sin = jnp.where(low, -turned, turn)

        def rotate(u):
            return (u * cos + pltpu.roll(u, HEAD_SIZE // 2, 1) * sin).astype(BF)

        key = rotate(both[:, width : width + HEAD_SIZE])
        value = both[:, width + HEAD_SIZE :].astype(BF)
        query = jnp.concatenate(
            [rotate(both[:, h * HEAD_SIZE : (h + 1) * HEAD_SIZE]) for h in range(heads)], axis=0
        )
        scores = lax.dot_general(
            query, key, (((1,), (1,)), ((), ())), preferred_element_type=F32
        ) * HEAD_SIZE ** (-0.5)
        scores = scores + jnp.concatenate([table[1, there, :]] * heads, axis=0)
        top = jnp.max(scores, axis=-1, keepdims=True)
        expo = jnp.exp(scores - top)
        probs = (expo / jnp.sum(expo, axis=-1, keepdims=True)).astype(BF)
        result = jnp.dot(probs, value, preferred_element_type=F32).astype(BF)
        for h in range(heads):
            out[here, h * HEAD_SIZE : (h + 1) * HEAD_SIZE] = result[
                h * ROW_TOKENS : (h + 1) * ROW_TOKENS
            ]


def attend(chunk, keep, near, across, squares, table):
    _, tokens, columns = keep.shape
    width = columns - 2 * HEAD_SIZE
    return pl.pallas_call(
        functools.partial(attend_kernel, chunk),
        in_specs=[VMEM] * 5,
        out_specs=VMEM,
        out_shape=jax.ShapeDtypeStruct((tokens, width), BF),
        name="attend",
        compiler_params=params(16),
        cost_estimate=cost(4 * tokens * width * ROW_TOKENS, 8 * tokens * columns),
    )(keep, near, across, squares, table)


def expand_kernel(steps, place, mine, other, weights, *outs):
    z, first = place[0], place[3]
    straight = first == 0
    left = jnp.where(straight, mine[...], other[...])
    right = jnp.where(straight, other[...], mine[...])
    wide = weights.shape[-1]
    for out, step in zip(outs, steps):
        block = 2 * lax.rem(z + step, 4)
        for k in range(2):
            total = jnp.dot(left, weights[block + k, 0], preferred_element_type=F32)
            total += jnp.dot(right, weights[block + k, 1], preferred_element_type=F32)
            out[:, k * wide : (k + 1) * wide] = total.astype(BF)


def expand(steps, place, mine, other, weights):
    tokens, depth = mine.shape
    wide = weights.shape[-1]
    count = len(steps)
    return pl.pallas_call(
        functools.partial(expand_kernel, steps),
        in_specs=[SMEM, VMEM, VMEM, VMEM],
        out_specs=[VMEM] * count,
        out_shape=[jax.ShapeDtypeStruct((tokens, 2 * wide), BF)] * count,
        name="expand",
        compiler_params=params(16),
        cost_estimate=cost(count * 8 * tokens * depth * wide, count * 3 * 1024 * 1024),
    )(place, mine, other, weights)


def after(values, *events):
    return lax.optimization_barrier((*values, *events))


def shift(x, axis, by):
    size = lax.axis_size(axis)
    return lax.ppermute(x, axis, [(i, (i + by) % size) for i in range(size)])


def spread(x):
    def at(place):
        return (place % 2) * 2 + place // 2

    first = [(0, 1), (1, 3), (2, 0), (3, 2)]
    second = [(0, 0), (1, 2), (2, 1), (3, 3)]
    return tuple(
        lax.ppermute(x, ("xl", "xh"), [(at(a), at(b)) for a, b in pairs])
        for pairs in (first, second)
    )


def row_mask(ids):
    pair_of = ids // 3
    role_of = ids % 3
    steps_a = jnp.arange(ids.shape[0])
    causal = steps_a[None, :] <= steps_a[:, None]
    same = pair_of[:, None] == pair_of[None, :]
    hidden_pair = (role_of[:, None] == 2) & (role_of[None, :] == 1)
    return causal & same & jnp.logical_not(hidden_pair)


def local(
    pair_tokens,
    norm_gain,
    q_weight,
    k_weight,
    value_weight,
    o_weight,
    pair_row,
    pair_span,
    block_ids,
):
    dp = ("xl", "y", "c")
    dp_count = lax.axis_size(dp)
    own = lax.axis_index(dp)
    xl, y, core = (lax.axis_index(a) for a in dp)
    xh, z = lax.axis_index("xh"), lax.axis_index("z")
    pairs_dev, pair_cap, width_local = pair_tokens.shape
    tok_dev = block_ids.shape[0]
    rows_dev = tok_dev // ROW_TOKENS
    first = jnp.where(xh == 1 - xl, 0, 1).astype(jnp.int32)

    owners_all = (pair_row // rows_dev).reshape(dp_count, pairs_dev)
    rows = q_weight.shape[0]
    gain = lax.dynamic_slice_in_dim(norm_gain, own * rows, rows, 0)[:, None]
    q_in = (q_weight.astype(F32) * gain).astype(BF)
    kv_in = jnp.concatenate([k_weight, value_weight], axis=1)
    kv_in = (kv_in.astype(F32) * gain).astype(BF)
    outgoing = dispatch(own.astype(jnp.int32), pair_row, pair_tokens, rows_dev)
    q_pair = spread(q_in)
    kv_blocks = (kv_in, shift(kv_in, "y", 1), shift(kv_in, "y", -1), shift(kv_in, "y", 2))
    outgoing = outgoing.reshape(dp_count, 2, pair_cap, width_local // 2)
    incoming = lax.all_to_all(outgoing, dp, split_axis=0, concat_axis=0, tiled=True)

    incoming = after((incoming,), *q_pair, *kv_blocks)[0]

    slots = jnp.arange(pair_cap, dtype=jnp.int32)
    begin = ((pair_row % rows_dev) * ROW_TOKENS + pair_span[:, 0]).reshape(dp_count, pairs_dev)
    length = (pair_span[:, 1] - pair_span[:, 0]).reshape(dp_count, pairs_dev)
    owner_here = (own // 2) * 2 + jnp.arange(2, dtype=jnp.int32)
    match = owners_all[None] == owner_here[:, None, None]
    begin_here = jnp.sum(jnp.where(match, begin[None], 0), axis=2)
    length_here = jnp.sum(jnp.where(match, length[None], 0), axis=2)
    target = jnp.where(
        slots[None, None, :] < length_here[:, :, None],
        begin_here[:, :, None] + slots[None, None, :],
        -1,
    ).reshape(2, dp_count * pair_cap)
    packed = pack(target, incoming, 2 * tok_dev)
    x_blocks = lax.all_gather(packed, "z", axis=0, tiled=False)

    q_both = jnp.stack(after(q_pair, packed)[:2])
    q_before, q_behind = shift(q_both, "y", 1), shift(q_both, "y", -1)
    kv_all = jnp.stack(after(kv_blocks, packed)[:4])
    kv_first, kv_second = spread(kv_all)
    q_from, q_back = after((q_before, q_behind), kv_first, kv_second)[:2]
    far_low, far_high = shift(q_from[0], "y", 1), shift(q_back[1], "y", -1)
    w_q = stage((q_both, q_before, q_behind))

    visible = jax.vmap(row_mask)(block_ids.reshape(rows_dev, ROW_TOKENS))
    position = (jnp.sum(visible.astype(jnp.int32), axis=2) - 1).reshape(tok_dev)
    half = HEAD_SIZE // 2
    freq = 500000.0 ** (-(jnp.arange(half, dtype=F32) * 2.0 / HEAD_SIZE))
    angle = position.astype(F32)[:, None] * freq[None, :]
    turns = jnp.concatenate([jnp.cos(angle), jnp.sin(angle)], axis=1)

    bias = jnp.where(visible, 0.0, -1e30).astype(F32).reshape(tok_dev, ROW_TOKENS)

    table = tables(turns, bias)

    o_in = after((o_weight,), q_from, q_back, table)[0]
    o_pair = after(spread(o_in), far_low, far_high)[:2]
    o_both = after((jnp.stack(o_pair),), x_blocks)[0]
    o_all = lax.all_gather(o_both, ("y", "c"), axis=0, tiled=False)

    place = jnp.stack([z, y, core, first]).astype(jnp.int32)
    place, table, w_q = lax.optimization_barrier((place, table, w_q))

    keeps, sends, squares = project(place, x_blocks, w_q, far_low, far_high, kv_first, kv_second)
    squares = squares.reshape(2, tok_dev // 128, 128)
    across_both = lax.ppermute(squares[0], ("c", "xh"), [(i, 3 - i) for i in range(4)])
    squares = (
        squares[1] + shift(squares[0], "c", 1) + shift(squares[1], "xh", 1) + across_both
    )
    nears = [shift(send, "c", 1) for send in sends]
    others = [(keep[1] + near[1].astype(F32)).astype(BF) for keep, near in zip(keeps, nears)]
    across_low = shift(others[0], "xh", 1)
    across_high = shift(after((others[1],), squares)[0], "xh", 1)
    acrosses = [across_low, across_high]
    mean = squares * (1.0 / norm_gain.shape[0])
    attns = [
        attend(chunk, keeps[chunk], nears[chunk], acrosses[chunk], mean, table)
        for chunk in range(CHUNKS)
    ]
    swapped = [shift(attn, "xh", 1) for attn in attns]
    o_all = after((o_all,), *swapped)[0]

    def terms(chunk, steps):
        return expand(steps, place, attns[chunk], swapped[chunk], o_all)

    far_low, down_low = terms(0, (2, 3))
    passing_low = shift(far_low, "z", 1)
    down_low = shift(down_low, "z", -1)
    far_high, up_high = terms(1, (2, 1))
    passing_high = shift(far_high, "z", -1)
    up_high = shift(up_high, "z", 1)
    up_low, own_low = terms(0, (1, 0))
    down_high, own_high = terms(1, (3, 0))
    up_low = shift((up_low.astype(F32) + passing_low.astype(F32)).astype(BF), "z", 1)
    down_high = shift((down_high.astype(F32) + passing_high.astype(F32)).astype(BF), "z", -1)
    low = own_low.astype(F32) + up_low.astype(F32) + down_low.astype(F32)
    high = own_high.astype(F32) + up_high.astype(F32) + down_high.astype(F32)
    return jnp.concatenate([low.astype(BF), high.astype(BF)], axis=0)


def solution(mesh):
    fine = Mesh(mesh.devices.reshape(2, 4, 2, 2, 4), ("xl", "y", "c", "xh", "z"))
    dp, mp = ("xl", "y", "c"), ("xh", "z")
    placed = (
        P(dp, None, mp),
        P(),
        P(dp, mp),
        P(dp, mp),
        P(dp, mp),
        P(mp, dp),
        P(),
        P(),
        P(dp),
    )
    return jax.shard_map(
        local, mesh=fine, in_specs=placed, out_specs=P(dp, mp), check_vma=False
    )
```

```python
import functools

import jax
import jax.numpy as jnp
from jax import lax
from jax.experimental import pallas as pl
from jax.experimental.pallas import tpu as pltpu
from jax.sharding import Mesh, PartitionSpec as P

HEAD_SIZE = 128
ROW_TOKENS = 128
QUERY_PER_KV = 4
BF = jnp.bfloat16
F32 = jnp.float32

VMEM = pl.BlockSpec(memory_space=pltpu.VMEM)
SMEM = pl.BlockSpec(memory_space=pltpu.SMEM)
ANY = pl.BlockSpec(memory_space=pl.ANY)
CHUNKS = 2
STEPS = (0, 3, 1, 2)


def params(mib):
    return pltpu.CompilerParams(vmem_limit_bytes=mib * 1024 * 1024)


def cost(flops, nbytes):
    return pl.CostEstimate(flops=flops, bytes_accessed=nbytes, transcendentals=0)


def dispatch_kernel(rows_dev, place, pair_row, pairs, out):
    count, _, width = pairs.shape
    half = width // 2
    for p in range(count):
        owner = lax.div(pair_row[place[0] * count + p], rows_dev)
        chip = lax.div(owner, 2)
        core = owner - 2 * chip
        for k in range(2):
            out[chip, k, core] = pairs[p, :, k * half : (k + 1) * half]


def dispatch(own, pair_row, pair_tokens, rows_dev):
    count, cap, width = pair_tokens.shape
    return pl.pallas_call(
        functools.partial(dispatch_kernel, rows_dev),
        in_specs=[SMEM, SMEM, VMEM],
        out_specs=VMEM,
        out_shape=jax.ShapeDtypeStruct((count // 2, 2, 2, cap, width // 2), BF),
        name="dispatch",
        compiler_params=params(60),
        cost_estimate=cost(0, 4 * count * cap * width),
    )(own.reshape(1), pair_row, pair_tokens)


def pack_kernel(target, incoming, packed):
    sources, cores, cap, width = incoming.shape
    rows = packed.shape[0] // cores
    for core in range(cores):
        slots = incoming[:, core].reshape(sources * cap, width)
        wanted = lax.broadcasted_iota(jnp.int32, (rows, sources * cap), 0)
        pick = (wanted == target[core : core + 1, :]).astype(F32).astype(BF)
        wide = jnp.dot(pick, slots, preferred_element_type=F32)
        packed[pl.ds(core * rows, rows), :] = wide.astype(BF)


def pack(target, incoming, rows):
    sources, cores, cap, width = incoming.shape
    return pl.pallas_call(
        pack_kernel,
        in_specs=[VMEM] * 2,
        out_specs=VMEM,
        out_shape=jax.ShapeDtypeStruct((rows, width), BF),
        name="pack",
        compiler_params=params(36),
        cost_estimate=cost(2 * rows * sources * cap * width, 4 * sources * cap * width),
    )(target, incoming)


def stage_kernel(*refs):
    sources, out, sems = refs[:-2], refs[-2], refs[-1]
    copies = [
        pltpu.make_async_copy(source, out.at[i], sems.at[i]) for i, source in enumerate(sources)
    ]
    for copy in copies:
        copy.start()
    for copy in copies:
        copy.wait()


def stage(sources):
    count = len(sources)
    return pl.pallas_call(
        stage_kernel,
        in_specs=[ANY] * count,
        out_specs=VMEM,
        out_shape=pltpu.VMEM((count, *sources[0].shape), BF),
        scratch_shapes=[pltpu.SemaphoreType.DMA((count,))],
        name="stage",
        compiler_params=params(16),
        cost_estimate=cost(0, 4 * count * sources[0].size),
    )(*sources)


def project_kernel(place, x, w_q, far_low, far_high, kv_first, kv_second, *refs):
    keeps, sends, squares = refs[:CHUNKS], refs[CHUNKS : 2 * CHUNKS], refs[2 * CHUNKS]
    y, core, first = place[1], place[2], place[3]
    rows = keeps[0].shape[1]
    span = rows * CHUNKS
    depth = x.shape[2]

    def split(value):
        low, high = value[:span], value[span:]
        return jnp.where(core == 0, high, low), jnp.where(core == 0, low, high)

    blocks = [lax.rem(y + step, 4) for step in STEPS]
    tile = 256
    wide = w_q.shape[3]
    for which in range(2):
        slot = first if which == 0 else 1 - first
        for begin in range(0, wide + kv_first.shape[2], tile):
            total = jnp.zeros((2 * span, tile), F32)
            for k in range(4):
                here = slice(begin, begin + tile)
                if begin >= wide:
                    piece = (kv_first, kv_second)[which][k, :, begin - wide : begin - wide + tile]
                elif k < 3:
                    piece = w_q[k, which, :, here]
                else:
                    piece = (far_low, far_high)[which][:, here]
                total += jnp.dot(x[blocks[k]], piece, preferred_element_type=F32)
            theirs, mine = split(total)
            for chunk in range(CHUNKS):
                lo = chunk * rows
                sends[chunk][slot, :, here] = theirs[lo : lo + rows].astype(BF)
                keeps[chunk][slot, :, here] = mine[lo : lo + rows]
    total = jnp.zeros((2 * span, depth), F32)
    for k in range(4):
        wide = x[k].astype(F32)
        total += wide * wide
    squares[0], squares[1] = split(jnp.sum(total, axis=1, keepdims=True))


def project(place, x, w_q, far_low, far_high, kv_first, kv_second):
    _, tokens, depth = x.shape
    span = tokens // 2
    columns = w_q.shape[3] + kv_first.shape[2]
    rows = span // CHUNKS
    results = pl.pallas_call(
        project_kernel,
        in_specs=[SMEM] + [VMEM] * 6,
        out_specs=[VMEM] * (2 * CHUNKS + 1),
        out_shape=[pltpu.VMEM((2, rows, columns), F32)] * CHUNKS
        + [jax.ShapeDtypeStruct((2, rows, columns), BF)] * CHUNKS
        + [jax.ShapeDtypeStruct((2, span, 1), F32)],
        name="project",
        compiler_params=params(24),
        cost_estimate=cost(4 * span * depth * 4 * columns * 2, 10 * 1024 * 1024),
    )(place, x, w_q, far_low, far_high, kv_first, kv_second)
    return results[:CHUNKS], results[CHUNKS : 2 * CHUNKS], results[2 * CHUNKS]


def tables_kernel(turns, bias, out):
    out[0] = turns[...]
    out[1] = bias[...]


def tables(turns, bias):
    return pl.pallas_call(
        tables_kernel,
        in_specs=[VMEM] * 2,
        out_specs=VMEM,
        out_shape=pltpu.VMEM((2, *turns.shape), F32),
        name="tables",
        compiler_params=params(16),
        cost_estimate=cost(0, 16 * turns.size),
    )(turns, bias)


def attend_kernel(chunk, keep, near, across, squares, table, out):
    tokens = out.shape[0]
    heads = out.shape[1] // HEAD_SIZE
    width = heads * HEAD_SIZE
    lane = lax.broadcasted_iota(jnp.int32, (ROW_TOKENS, HEAD_SIZE), 1)
    low = lane < HEAD_SIZE // 2
    diagonal = lane == lax.broadcasted_iota(jnp.int32, (ROW_TOKENS, HEAD_SIZE), 0)
    for r in range(tokens // ROW_TOKENS):
        here = slice(r * ROW_TOKENS, (r + 1) * ROW_TOKENS)
        row = chunk * (tokens // ROW_TOKENS) + r
        there = slice(row * ROW_TOKENS, (row + 1) * ROW_TOKENS)
        column = jnp.sum(jnp.where(diagonal, squares[row : row + 1, :], 0.0), axis=1, keepdims=True)
        scale = lax.rsqrt(column + 1e-05)
        both = keep[0, here, :] + near[0, here, :].astype(F32) + across[here, :].astype(F32)
        both = both * scale
        turn = table[0, there, :]
        turned = pltpu.roll(turn, HEAD_SIZE // 2, 1)
        cos = jnp.where(low, turn, turned)
        sin = jnp.where(low, -turned, turn)

        def rotate(u):
            return (u * cos + pltpu.roll(u, HEAD_SIZE // 2, 1) * sin).astype(BF)

        key = rotate(both[:, width : width + HEAD_SIZE])
        value = both[:, width + HEAD_SIZE :].astype(BF)
        query = jnp.concatenate(
            [rotate(both[:, h * HEAD_SIZE : (h + 1) * HEAD_SIZE]) for h in range(heads)], axis=0
        )
        scores = lax.dot_general(
            query, key, (((1,), (1,)), ((), ())), preferred_element_type=F32
        ) * HEAD_SIZE ** (-0.5)
        scores = scores + jnp.concatenate([table[1, there, :]] * heads, axis=0)
        top = jnp.max(scores, axis=-1, keepdims=True)
        expo = jnp.exp(scores - top)
        probs = (expo / jnp.sum(expo, axis=-1, keepdims=True)).astype(BF)
        result = jnp.dot(probs, value, preferred_element_type=F32).astype(BF)
        for h in range(heads):
            out[here, h * HEAD_SIZE : (h + 1) * HEAD_SIZE] = result[
                h * ROW_TOKENS : (h + 1) * ROW_TOKENS
            ]


def attend(chunk, keep, near, across, squares, table):
    _, tokens, columns = keep.shape
    width = columns - 2 * HEAD_SIZE
    return pl.pallas_call(
        functools.partial(attend_kernel, chunk),
        in_specs=[VMEM] * 5,
        out_specs=VMEM,
        out_shape=jax.ShapeDtypeStruct((tokens, width), BF),
        name="attend",
        compiler_params=params(16),
        cost_estimate=cost(4 * tokens * width * ROW_TOKENS, 8 * tokens * columns),
    )(keep, near, across, squares, table)


def expand_kernel(steps, place, *refs):
    pairs, weights, outs = (refs[0:2], refs[2:4]), refs[4], refs[5:]
    z, first = place[0], place[3]
    straight = first == 0
    wide = weights.shape[-1]
    outs = iter(outs)
    for (mine, other), chosen in zip(pairs, steps):
        left = jnp.where(straight, mine[...], other[...])
        right = jnp.where(straight, other[...], mine[...])
        for step in chosen:
            out = next(outs)
            block = 2 * lax.rem(z + step, 4)
            for k in range(2):
                total = jnp.dot(left, weights[block + k, 0], preferred_element_type=F32)
                total += jnp.dot(right, weights[block + k, 1], preferred_element_type=F32)
                out[:, k * wide : (k + 1) * wide] = total.astype(BF)


def expand(steps, place, attns, swapped, weights):
    tokens, depth = attns[0].shape
    wide = weights.shape[-1]
    count = sum(len(chosen) for chosen in steps)
    return pl.pallas_call(
        functools.partial(expand_kernel, steps),
        in_specs=[SMEM] + [VMEM] * 5,
        out_specs=[VMEM] * count,
        out_shape=[jax.ShapeDtypeStruct((tokens, 2 * wide), BF)] * count,
        name="expand",
        compiler_params=params(16),
        cost_estimate=cost(count * 8 * tokens * depth * wide, count * 3 * 1024 * 1024),
    )(place, attns[0], swapped[0], attns[1], swapped[1], weights)


def after(values, *events):
    return lax.optimization_barrier((*values, *events))


def shift(x, axis, by):
    size = lax.axis_size(axis)
    return lax.ppermute(x, axis, [(i, (i + by) % size) for i in range(size)])


def spread(x):
    def at(place):
        return (place % 2) * 2 + place // 2

    first = [(0, 1), (1, 3), (2, 0), (3, 2)]
    second = [(0, 0), (1, 2), (2, 1), (3, 3)]
    return tuple(
        lax.ppermute(x, ("xl", "xh"), [(at(a), at(b)) for a, b in pairs])
        for pairs in (first, second)
    )


def row_mask(ids):
    pair_of = ids // 3
    role_of = ids % 3
    steps_a = jnp.arange(ids.shape[0])
    causal = steps_a[None, :] <= steps_a[:, None]
    same = pair_of[:, None] == pair_of[None, :]
    hidden_pair = (role_of[:, None] == 2) & (role_of[None, :] == 1)
    return causal & same & jnp.logical_not(hidden_pair)


def local(
    pair_tokens,
    norm_gain,
    q_weight,
    k_weight,
    value_weight,
    o_weight,
    pair_row,
    pair_span,
    block_ids,
):
    dp = ("xl", "y", "c")
    dp_count = lax.axis_size(dp)
    own = lax.axis_index(dp)
    xl, y, core = (lax.axis_index(a) for a in dp)
    xh, z = lax.axis_index("xh"), lax.axis_index("z")
    pairs_dev, pair_cap, width_local = pair_tokens.shape
    tok_dev = block_ids.shape[0]
    rows_dev = tok_dev // ROW_TOKENS
    first = jnp.where(xh == 1 - xl, 0, 1).astype(jnp.int32)

    owners_all = (pair_row // rows_dev).reshape(dp_count, pairs_dev)
    rows = q_weight.shape[0]
    gain = lax.dynamic_slice_in_dim(norm_gain, own * rows, rows, 0)[:, None]
    q_in = (q_weight.astype(F32) * gain).astype(BF)
    kv_in = jnp.concatenate([k_weight, value_weight], axis=1)
    kv_in = (kv_in.astype(F32) * gain).astype(BF)
    outgoing = dispatch(own.astype(jnp.int32), pair_row, pair_tokens, rows_dev)
    q_pair = spread(q_in)
    kv_blocks = (kv_in, shift(kv_in, "y", 1), shift(kv_in, "y", -1), shift(kv_in, "y", 2))
    outgoing = outgoing.reshape(dp_count, 2, pair_cap, width_local // 2)
    incoming = lax.all_to_all(outgoing, dp, split_axis=0, concat_axis=0, tiled=True)

    incoming = after((incoming,), *q_pair, *kv_blocks)[0]

    slots = jnp.arange(pair_cap, dtype=jnp.int32)
    begin = ((pair_row % rows_dev) * ROW_TOKENS + pair_span[:, 0]).reshape(dp_count, pairs_dev)
    length = (pair_span[:, 1] - pair_span[:, 0]).reshape(dp_count, pairs_dev)
    owner_here = (own // 2) * 2 + jnp.arange(2, dtype=jnp.int32)
    match = owners_all[None] == owner_here[:, None, None]
    begin_here = jnp.sum(jnp.where(match, begin[None], 0), axis=2)
    length_here = jnp.sum(jnp.where(match, length[None], 0), axis=2)
    target = jnp.where(
        slots[None, None, :] < length_here[:, :, None],
        begin_here[:, :, None] + slots[None, None, :],
        -1,
    ).reshape(2, dp_count * pair_cap)
    packed = pack(target, incoming, 2 * tok_dev)
    x_blocks = lax.all_gather(packed, "z", axis=0, tiled=False)

    q_both = jnp.stack(after(q_pair, packed)[:2])
    q_before, q_behind = shift(q_both, "y", 1), shift(q_both, "y", -1)
    kv_all = jnp.stack(after(kv_blocks, packed)[:4])
    kv_first, kv_second = spread(kv_all)
    q_from, q_back = after((q_before, q_behind), kv_first, kv_second)[:2]
    far_low, far_high = shift(q_from[0], "y", 1), shift(q_back[1], "y", -1)
    w_q = stage((q_both, q_before, q_behind))

    visible = jax.vmap(row_mask)(block_ids.reshape(rows_dev, ROW_TOKENS))
    position = (jnp.sum(visible.astype(jnp.int32), axis=2) - 1).reshape(tok_dev)
    half = HEAD_SIZE // 2
    freq = 500000.0 ** (-(jnp.arange(half, dtype=F32) * 2.0 / HEAD_SIZE))
    angle = position.astype(F32)[:, None] * freq[None, :]
    turns = jnp.concatenate([jnp.cos(angle), jnp.sin(angle)], axis=1)

    bias = jnp.where(visible, 0.0, -1e30).astype(F32).reshape(tok_dev, ROW_TOKENS)

    table = tables(turns, bias)

    o_in = after((o_weight,), q_from, q_back, table)[0]
    o_pair = after(spread(o_in), far_low, far_high)[:2]
    o_both = after((jnp.stack(o_pair),), x_blocks)[0]
    o_all = lax.all_gather(o_both, ("y", "c"), axis=0, tiled=False)

    place = jnp.stack([z, y, core, first]).astype(jnp.int32)
    place, table, w_q = lax.optimization_barrier((place, table, w_q))

    keeps, sends, squares = project(place, x_blocks, w_q, far_low, far_high, kv_first, kv_second)
    squares = squares.reshape(2, tok_dev // 128, 128)
    across_both = lax.ppermute(squares[0], ("c", "xh"), [(i, 3 - i) for i in range(4)])
    squares = (
        squares[1] + shift(squares[0], "c", 1) + shift(squares[1], "xh", 1) + across_both
    )
    nears = [shift(send, "c", 1) for send in sends]
    others = [(keep[1] + near[1].astype(F32)).astype(BF) for keep, near in zip(keeps, nears)]
    across_low = shift(others[0], "xh", 1)
    across_high = shift(after((others[1],), squares)[0], "xh", 1)
    acrosses = [across_low, across_high]
    mean = squares * (1.0 / norm_gain.shape[0])
    attns = [
        attend(chunk, keeps[chunk], nears[chunk], acrosses[chunk], mean, table)
        for chunk in range(CHUNKS)
    ]
    swapped = [shift(attn, "xh", 1) for attn in attns]
    o_all = after((o_all,), *swapped)[0]

    far_low, far_high = expand(((2,), (2,)), place, attns, swapped, o_all)
    passing_low = shift(far_low, "z", 1)
    passing_high = shift(far_high, "z", -1)
    o_late = after((o_all,), far_low, far_high)[0]
    down_low, up_low, own_low, up_high, down_high, own_high = expand(
        ((3, 1, 0), (1, 3, 0)), place, attns, swapped, o_late
    )
    down_low = shift(down_low, "z", -1)
    up_high = shift(up_high, "z", 1)
    up_low = shift((up_low.astype(F32) + passing_low.astype(F32)).astype(BF), "z", 1)
    down_high = shift((down_high.astype(F32) + passing_high.astype(F32)).astype(BF), "z", -1)
    low = own_low.astype(F32) + up_low.astype(F32) + down_low.astype(F32)
    high = own_high.astype(F32) + up_high.astype(F32) + down_high.astype(F32)
    return jnp.concatenate([low.astype(BF), high.astype(BF)], axis=0)


def solution(mesh):
    fine = Mesh(mesh.devices.reshape(2, 4, 2, 2, 4), ("xl", "y", "c", "xh", "z"))
    dp, mp = ("xl", "y", "c"), ("xh", "z")
    placed = (
        P(dp, None, mp),
        P(),
        P(dp, mp),
        P(dp, mp),
        P(dp, mp),
        P(mp, dp),
        P(),
        P(),
        P(dp),
    )
    return jax.shard_map(
        local, mesh=fine, in_specs=placed, out_specs=P(dp, mp), check_vma=False
    )
```

```python
import functools

import jax
import jax.numpy as jnp
from jax import lax
from jax.experimental import pallas as pl
from jax.experimental.pallas import tpu as pltpu
from jax.sharding import Mesh, PartitionSpec as P

HEAD_SIZE = 128
ROW_TOKENS = 128
QUERY_PER_KV = 4
BF = jnp.bfloat16
F32 = jnp.float32

VMEM = pl.BlockSpec(memory_space=pltpu.VMEM)
SMEM = pl.BlockSpec(memory_space=pltpu.SMEM)
ANY = pl.BlockSpec(memory_space=pl.ANY)
CHUNKS = 2
STEPS = (0, 3, 1, 2)


def params(mib):
    return pltpu.CompilerParams(vmem_limit_bytes=mib * 1024 * 1024)


def cost(flops, nbytes):
    return pl.CostEstimate(flops=flops, bytes_accessed=nbytes, transcendentals=0)


def dispatch_kernel(rows_dev, place, pair_row, pairs, out):
    count, _, width = pairs.shape
    half = width // 2
    for p in range(count):
        owner = lax.div(pair_row[place[0] * count + p], rows_dev)
        chip = lax.div(owner, 2)
        core = owner - 2 * chip
        for k in range(2):
            out[chip, k, core] = pairs[p, :, k * half : (k + 1) * half]


def dispatch(own, pair_row, pair_tokens, rows_dev):
    count, cap, width = pair_tokens.shape
    return pl.pallas_call(
        functools.partial(dispatch_kernel, rows_dev),
        in_specs=[SMEM, SMEM, VMEM],
        out_specs=VMEM,
        out_shape=jax.ShapeDtypeStruct((count // 2, 2, 2, cap, width // 2), BF),
        name="dispatch",
        compiler_params=params(60),
        cost_estimate=cost(0, 4 * count * cap * width),
    )(own.reshape(1), pair_row, pair_tokens)


def pack_kernel(target, incoming, packed):
    sources, cores, cap, width = incoming.shape
    rows = packed.shape[0] // cores
    for core in range(cores):
        slots = incoming[:, core].reshape(sources * cap, width)
        wanted = lax.broadcasted_iota(jnp.int32, (rows, sources * cap), 0)
        pick = (wanted == target[core : core + 1, :]).astype(F32).astype(BF)
        wide = jnp.dot(pick, slots, preferred_element_type=F32)
        packed[pl.ds(core * rows, rows), :] = wide.astype(BF)


def pack(target, incoming, rows):
    sources, cores, cap, width = incoming.shape
    return pl.pallas_call(
        pack_kernel,
        in_specs=[VMEM] * 2,
        out_specs=VMEM,
        out_shape=jax.ShapeDtypeStruct((rows, width), BF),
        name="pack",
        compiler_params=params(36),
        cost_estimate=cost(2 * rows * sources * cap * width, 4 * sources * cap * width),
    )(target, incoming)


def stage_kernel(*refs):
    sources, out, sems = refs[:-2], refs[-2], refs[-1]
    copies = [
        pltpu.make_async_copy(source, out.at[i], sems.at[i]) for i, source in enumerate(sources)
    ]
    for copy in copies:
        copy.start()
    for copy in copies:
        copy.wait()


def stage(sources):
    count = len(sources)
    return pl.pallas_call(
        stage_kernel,
        in_specs=[ANY] * count,
        out_specs=VMEM,
        out_shape=pltpu.VMEM((count, *sources[0].shape), BF),
        scratch_shapes=[pltpu.SemaphoreType.DMA((count,))],
        name="stage",
        compiler_params=params(16),
        cost_estimate=cost(0, 4 * count * sources[0].size),
    )(*sources)


def project_kernel(place, x, w_q, far_low, far_high, kv_first, kv_second, *refs):
    keeps, sends, squares = refs[:CHUNKS], refs[CHUNKS : 2 * CHUNKS], refs[2 * CHUNKS]
    y, core, first = place[1], place[2], place[3]
    rows = keeps[0].shape[1]
    span = rows * CHUNKS
    depth = x.shape[2]

    def split(value):
        low, high = value[:span], value[span:]
        return jnp.where(core == 0, high, low), jnp.where(core == 0, low, high)

    blocks = [lax.rem(y + step, 4) for step in STEPS]
    tile = 256
    wide = w_q.shape[3]
    for which in range(2):
        slot = first if which == 0 else 1 - first
        for begin in range(0, wide + kv_first.shape[2], tile):
            total = jnp.zeros((2 * span, tile), F32)
            for k in range(4):
                here = slice(begin, begin + tile)
                if begin >= wide:
                    piece = (kv_first, kv_second)[which][k, :, begin - wide : begin - wide + tile]
                elif k < 3:
                    piece = w_q[k, which, :, here]
                else:
                    piece = (far_low, far_high)[which][:, here]
                total += jnp.dot(x[blocks[k]], piece, preferred_element_type=F32)
            theirs, mine = split(total)
            for chunk in range(CHUNKS):
                lo = chunk * rows
                sends[chunk][slot, :, here] = theirs[lo : lo + rows].astype(BF)
                keeps[chunk][slot, :, here] = mine[lo : lo + rows]
    total = jnp.zeros((2 * span, depth), F32)
    for k in range(4):
        wide = x[k].astype(F32)
        total += wide * wide
    squares[0], squares[1] = split(jnp.sum(total, axis=1, keepdims=True))


def project(place, x, w_q, far_low, far_high, kv_first, kv_second):
    _, tokens, depth = x.shape
    span = tokens // 2
    columns = w_q.shape[3] + kv_first.shape[2]
    rows = span // CHUNKS
    results = pl.pallas_call(
        project_kernel,
        in_specs=[SMEM] + [VMEM] * 6,
        out_specs=[VMEM] * (2 * CHUNKS + 1),
        out_shape=[pltpu.VMEM((2, rows, columns), F32)] * CHUNKS
        + [jax.ShapeDtypeStruct((2, rows, columns), BF)] * CHUNKS
        + [jax.ShapeDtypeStruct((2, span, 1), F32)],
        name="project",
        compiler_params=params(24),
        cost_estimate=cost(4 * span * depth * 4 * columns * 2, 10 * 1024 * 1024),
    )(place, x, w_q, far_low, far_high, kv_first, kv_second)
    return results[:CHUNKS], results[CHUNKS : 2 * CHUNKS], results[2 * CHUNKS]


def tables_kernel(turns, bias, out):
    out[0] = turns[...]
    out[1] = bias[...]


def tables(turns, bias):
    return pl.pallas_call(
        tables_kernel,
        in_specs=[VMEM] * 2,
        out_specs=VMEM,
        out_shape=pltpu.VMEM((2, *turns.shape), F32),
        name="tables",
        compiler_params=params(16),
        cost_estimate=cost(0, 16 * turns.size),
    )(turns, bias)


def attend_kernel(chunk, keep, near, across, squares, table, out):
    tokens = out.shape[0]
    heads = out.shape[1] // HEAD_SIZE
    width = heads * HEAD_SIZE
    lane = lax.broadcasted_iota(jnp.int32, (ROW_TOKENS, HEAD_SIZE), 1)
    low = lane < HEAD_SIZE // 2
    diagonal = lane == lax.broadcasted_iota(jnp.int32, (ROW_TOKENS, HEAD_SIZE), 0)
    for r in range(tokens // ROW_TOKENS):
        here = slice(r * ROW_TOKENS, (r + 1) * ROW_TOKENS)
        row = chunk * (tokens // ROW_TOKENS) + r
        there = slice(row * ROW_TOKENS, (row + 1) * ROW_TOKENS)
        column = jnp.sum(jnp.where(diagonal, squares[row : row + 1, :], 0.0), axis=1, keepdims=True)
        scale = lax.rsqrt(column + 1e-05)
        both = keep[0, here, :] + near[0, here, :].astype(F32) + across[here, :].astype(F32)
        both = both * scale
        turn = table[0, there, :]
        turned = pltpu.roll(turn, HEAD_SIZE // 2, 1)
        cos = jnp.where(low, turn, turned)
        sin = jnp.where(low, -turned, turn)

        def rotate(u):
            return (u * cos + pltpu.roll(u, HEAD_SIZE // 2, 1) * sin).astype(BF)

        key = rotate(both[:, width : width + HEAD_SIZE])
        value = both[:, width + HEAD_SIZE :].astype(BF)
        query = jnp.concatenate(
            [rotate(both[:, h * HEAD_SIZE : (h + 1) * HEAD_SIZE]) for h in range(heads)], axis=0
        )
        scores = lax.dot_general(
            query, key, (((1,), (1,)), ((), ())), preferred_element_type=F32
        ) * HEAD_SIZE ** (-0.5)
        scores = scores + jnp.concatenate([table[1, there, :]] * heads, axis=0)
        top = jnp.max(scores, axis=-1, keepdims=True)
        expo = jnp.exp(scores - top)
        probs = (expo / jnp.sum(expo, axis=-1, keepdims=True)).astype(BF)
        result = jnp.dot(probs, value, preferred_element_type=F32).astype(BF)
        for h in range(heads):
            out[here, h * HEAD_SIZE : (h + 1) * HEAD_SIZE] = result[
                h * ROW_TOKENS : (h + 1) * ROW_TOKENS
            ]


def attend(chunk, keep, near, across, squares, table):
    _, tokens, columns = keep.shape
    width = columns - 2 * HEAD_SIZE
    return pl.pallas_call(
        functools.partial(attend_kernel, chunk),
        in_specs=[VMEM] * 5,
        out_specs=VMEM,
        out_shape=jax.ShapeDtypeStruct((tokens, width), BF),
        name="attend",
        compiler_params=params(16),
        cost_estimate=cost(4 * tokens * width * ROW_TOKENS, 8 * tokens * columns),
    )(keep, near, across, squares, table)


def expand_kernel(steps, place, *refs):
    pairs, weights, outs = (refs[0:2], refs[2:4]), refs[4], refs[5:]
    z, first = place[0], place[3]
    straight = first == 0
    wide = weights.shape[-1]
    outs = iter(outs)
    for (mine, other), chosen in zip(pairs, steps):
        left = jnp.where(straight, mine[...], other[...])
        right = jnp.where(straight, other[...], mine[...])
        for step in chosen:
            out = next(outs)
            block = 2 * lax.rem(z + step, 4)
            for k in range(2):
                total = jnp.dot(left, weights[block + k, 0], preferred_element_type=F32)
                total += jnp.dot(right, weights[block + k, 1], preferred_element_type=F32)
                out[:, k * wide : (k + 1) * wide] = total.astype(BF)


def expand(steps, place, attns, swapped, weights):
    tokens, depth = attns[0].shape
    wide = weights.shape[-1]
    count = sum(len(chosen) for chosen in steps)
    return pl.pallas_call(
        functools.partial(expand_kernel, steps),
        in_specs=[SMEM] + [VMEM] * 5,
        out_specs=[VMEM] * count,
        out_shape=[jax.ShapeDtypeStruct((tokens, 2 * wide), BF)] * count,
        name="expand",
        compiler_params=params(16),
        cost_estimate=cost(count * 8 * tokens * depth * wide, count * 3 * 1024 * 1024),
    )(place, attns[0], swapped[0], attns[1], swapped[1], weights)


def after(values, *events):
    return lax.optimization_barrier((*values, *events))


def shift(x, axis, by):
    size = lax.axis_size(axis)
    return lax.ppermute(x, axis, [(i, (i + by) % size) for i in range(size)])


def spread(x):
    def at(place):
        return (place % 2) * 2 + place // 2

    first = [(0, 1), (1, 3), (2, 0), (3, 2)]
    second = [(0, 0), (1, 2), (2, 1), (3, 3)]
    return tuple(
        lax.ppermute(x, ("xl", "xh"), [(at(a), at(b)) for a, b in pairs])
        for pairs in (first, second)
    )


def row_mask(ids):
    pair_of = ids // 3
    role_of = ids % 3
    steps_a = jnp.arange(ids.shape[0])
    causal = steps_a[None, :] <= steps_a[:, None]
    same = pair_of[:, None] == pair_of[None, :]
    hidden_pair = (role_of[:, None] == 2) & (role_of[None, :] == 1)
    return causal & same & jnp.logical_not(hidden_pair)


def local(
    pair_tokens,
    norm_gain,
    q_weight,
    k_weight,
    value_weight,
    o_weight,
    pair_row,
    pair_span,
    block_ids,
):
    dp = ("xl", "y", "c")
    dp_count = lax.axis_size(dp)
    own = lax.axis_index(dp)
    xl, y, core = (lax.axis_index(a) for a in dp)
    xh, z = lax.axis_index("xh"), lax.axis_index("z")
    pairs_dev, pair_cap, width_local = pair_tokens.shape
    tok_dev = block_ids.shape[0]
    rows_dev = tok_dev // ROW_TOKENS
    first = jnp.where(xh == 1 - xl, 0, 1).astype(jnp.int32)

    owners_all = (pair_row // rows_dev).reshape(dp_count, pairs_dev)
    rows = q_weight.shape[0]
    gain = lax.dynamic_slice_in_dim(norm_gain, own * rows, rows, 0)[:, None]
    q_in = (q_weight.astype(F32) * gain).astype(BF)
    kv_in = jnp.concatenate([k_weight, value_weight], axis=1)
    kv_in = (kv_in.astype(F32) * gain).astype(BF)
    outgoing = dispatch(own.astype(jnp.int32), pair_row, pair_tokens, rows_dev)
    q_pair = spread(q_in)
    kv_blocks = (kv_in, shift(kv_in, "y", 1), shift(kv_in, "y", -1), shift(kv_in, "y", 2))
    outgoing = outgoing.reshape(dp_count, 2, pair_cap, width_local // 2)
    incoming = lax.all_to_all(outgoing, dp, split_axis=0, concat_axis=0, tiled=True)

    incoming = after((incoming,), *q_pair, *kv_blocks)[0]

    slots = jnp.arange(pair_cap, dtype=jnp.int32)
    begin = ((pair_row % rows_dev) * ROW_TOKENS + pair_span[:, 0]).reshape(dp_count, pairs_dev)
    length = (pair_span[:, 1] - pair_span[:, 0]).reshape(dp_count, pairs_dev)
    owner_here = (own // 2) * 2 + jnp.arange(2, dtype=jnp.int32)
    match = owners_all[None] == owner_here[:, None, None]
    begin_here = jnp.sum(jnp.where(match, begin[None], 0), axis=2)
    length_here = jnp.sum(jnp.where(match, length[None], 0), axis=2)
    target = jnp.where(
        slots[None, None, :] < length_here[:, :, None],
        begin_here[:, :, None] + slots[None, None, :],
        -1,
    ).reshape(2, dp_count * pair_cap)
    packed = pack(target, incoming, 2 * tok_dev)
    x_blocks = lax.all_gather(packed, "z", axis=0, tiled=False)

    q_both = jnp.stack(after(q_pair, packed)[:2])
    q_before, q_behind = shift(q_both, "y", 1), shift(q_both, "y", -1)
    kv_all = jnp.stack(after(kv_blocks, packed)[:4])
    kv_first, kv_second = spread(kv_all)
    q_from, q_back = after((q_before, q_behind), kv_first, kv_second)[:2]
    far_low, far_high = shift(q_from[0], "y", 1), shift(q_back[1], "y", -1)
    w_q = stage((q_both, q_before, q_behind))

    visible = jax.vmap(row_mask)(block_ids.reshape(rows_dev, ROW_TOKENS))
    position = (jnp.sum(visible.astype(jnp.int32), axis=2) - 1).reshape(tok_dev)
    half = HEAD_SIZE // 2
    freq = 500000.0 ** (-(jnp.arange(half, dtype=F32) * 2.0 / HEAD_SIZE))
    angle = position.astype(F32)[:, None] * freq[None, :]
    turns = jnp.concatenate([jnp.cos(angle), jnp.sin(angle)], axis=1)

    bias = jnp.where(visible, 0.0, -1e30).astype(F32).reshape(tok_dev, ROW_TOKENS)

    table = tables(turns, bias)

    o_in = after((o_weight,), q_from, q_back, table)[0]
    o_pair = after(spread(o_in), far_low, far_high)[:2]
    o_both = after((jnp.stack(o_pair),), x_blocks)[0]
    o_all = lax.all_gather(o_both, ("y", "c"), axis=0, tiled=False)

    place = jnp.stack([z, y, core, first]).astype(jnp.int32)
    place, table, w_q = lax.optimization_barrier((place, table, w_q))

    keeps, sends, squares = project(place, x_blocks, w_q, far_low, far_high, kv_first, kv_second)
    squares = squares.reshape(2, tok_dev // 128, 128)
    across_both = lax.ppermute(squares[0], ("c", "xh"), [(i, 3 - i) for i in range(4)])
    squares = (
        squares[1] + shift(squares[0], "c", 1) + shift(squares[1], "xh", 1) + across_both
    )
    nears = [shift(send, "c", 1) for send in sends]
    others = [(keep[1] + near[1].astype(F32)).astype(BF) for keep, near in zip(keeps, nears)]
    across_low = shift(others[0], "xh", 1)
    across_high = shift(after((others[1],), squares, across_low)[0], "xh", 1)
    acrosses = [across_low, across_high]
    mean = squares * (1.0 / norm_gain.shape[0])
    attns = [
        attend(chunk, keeps[chunk], nears[chunk], acrosses[chunk], mean, table)
        for chunk in range(CHUNKS)
    ]
    swapped = [shift(attn, "xh", 1) for attn in attns]
    o_all = after((o_all,), *swapped)[0]

    far_low, far_high = expand(((2,), (2,)), place, attns, swapped, o_all)
    passing_low = shift(far_low, "z", 1)
    passing_high = shift(far_high, "z", -1)
    o_late = after((o_all,), far_low, far_high)[0]
    down_low, up_low, own_low, up_high, down_high, own_high = expand(
        ((3, 1, 0), (1, 3, 0)), place, attns, swapped, o_late
    )
    down_low = shift(down_low, "z", -1)
    up_high = shift(up_high, "z", 1)
    up_low = shift((up_low.astype(F32) + passing_low.astype(F32)).astype(BF), "z", 1)
    down_high = shift((down_high.astype(F32) + passing_high.astype(F32)).astype(BF), "z", -1)
    low = own_low.astype(F32) + up_low.astype(F32) + down_low.astype(F32)
    high = own_high.astype(F32) + up_high.astype(F32) + down_high.astype(F32)
    return jnp.concatenate([low.astype(BF), high.astype(BF)], axis=0)


def solution(mesh):
    fine = Mesh(mesh.devices.reshape(2, 4, 2, 2, 4), ("xl", "y", "c", "xh", "z"))
    dp, mp = ("xl", "y", "c"), ("xh", "z")
    placed = (
        P(dp, None, mp),
        P(),
        P(dp, mp),
        P(dp, mp),
        P(dp, mp),
        P(mp, dp),
        P(),
        P(),
        P(dp),
    )
    return jax.shard_map(
        local, mesh=fine, in_specs=placed, out_specs=P(dp, mp), check_vma=False
    )
```
